512 devices in a mesh: row: 32 (over z, x_hi), col: 16 (over y, x_lo, core).
Axes of the slice: x: 4 (x_hi: 2, x_lo: 2; x = x_hi * 2 + x_lo), y: 4, z: 16, core: 2. Of those that a mesh axis runs over, the one named last changes fastest.
Arguments:
- merged_vectors: float32 [512, 102400], P('col', 'row'), may hold values from -6 to 6
- deflation: int32 [512], replicated, may hold values from 0 to 511, as said below
- vectors: float32 [4, 102400, 256], P(None, ('row', 'col')), may hold values from -0.0390625 to 0.0390625
- factors: float32 [4, 256, 256], replicated, may hold values from -0.25 to 2, as said below
Outputs:
- eigenvectors: float32 [512, 102400], P('col', 'row')
The draws below stay inside these ranges and needn't reach their ends.
Inputs may be any that keep to these rules, and one draw needn't show every extreme that they name: deflation is a permutation of the 512 eigenvectors; of the 32 eigenvectors held by one index of col, at most 4 are bound for any one index of col, and in every draw every index of col receives exactly 4 from some index. Each factors[b] is upper triangular.
All inputs are finite; a program needn't handle non-finite values.
Results may differ from the reference program's by a relative error of at most 0.0003.
Values sent between devices are 32-bit elements; how exact they have to be, the bound alone decides.
A program may use at most 128 MiB of HBM per device.

```python
import math
import jax
import jax.numpy as jnp
from jax import lax

N = 102400
NB = 256
BLOCKS = 4
K_DEV = 32
K = 512


def draw_deflation(key, part):
    key = jax.random.fold_in(key, 11)
    keys = jax.random.split(key, 4)
    groups_all = K // K_DEV
    capacity = 2 * K_DEV // groups_all
    offset = jax.random.randint(keys[0], (), 0, groups_all)
    shuffled = jax.random.permutation(keys[1], (groups_all - 1) * capacity)[:K_DEV - capacity]
    group_ids = shuffled // capacity + 1
    labels = jnp.arange(groups_all, dtype=jnp.int32)
    counts = jnp.sum((group_ids[:, None] == labels[None, :]).astype(jnp.int32), axis=0)
    counts = counts + capacity * (labels == 0).astype(jnp.int32)
    bounds = jnp.cumsum(counts)
    slot_index = jnp.arange(K_DEV, dtype=jnp.int32)
    group_of = jnp.sum((slot_index[:, None] >= bounds[None, :]).astype(jnp.int32), axis=1)
    shift_of = (group_of + offset) % groups_all
    source_dev = (labels[:, None] - shift_of[None, :]) % groups_all
    row_perms = jax.vmap(lambda sub: jax.random.permutation(sub, K_DEV))(jax.random.split(keys[2], groups_all))
    source_row = row_perms[source_dev, slot_index[None, :]]
    table = source_dev * K_DEV + source_row
    slot_perms = jax.vmap(lambda sub: jax.random.permutation(sub, K_DEV))(jax.random.split(keys[3], groups_all))
    return jnp.take_along_axis(table, slot_perms, axis=1).reshape(K).astype(jnp.int32)


def draw_factors(key, part):
    key = jax.random.fold_in(key, 7)
    key_diag, key_off = jax.random.split(key)
    diagonal = jax.random.uniform(key_diag, (BLOCKS, NB), jnp.float32, 1.0, 2.0)
    offside = jnp.clip(jax.random.normal(key_off, (BLOCKS, NB, NB), jnp.float32), -4.0, 4.0)
    offside = jnp.clip(offside / math.sqrt(NB), -0.25, 0.25)
    row_ids = lax.broadcasted_iota(jnp.int32, (NB, NB), 0)
    col_ids = lax.broadcasted_iota(jnp.int32, (NB, NB), 1)
    strict = jnp.where((col_ids > row_ids)[None, :, :], offside, 0.0)
    return strict + jnp.where((col_ids == row_ids)[None, :, :], diagonal[:, :, None], 0.0)


def steps_of(rng, dims, cuts, low, largest):
    level = 1.0
    for position, parts in cuts:
        draws = jax.random.uniform(jax.random.fold_in(jax.random.fold_in(rng, 6), position), (parts,), jnp.float32, low / len(cuts), largest / len(cuts))
        level = level * jnp.repeat(jnp.exp(draws), dims[position] // parts).reshape((-1,) + (1,) * (len(dims) - 1 - position))
    return level


def bell_draw(rng, dims, deviation, bound, shards=(), kind=jnp.bfloat16):
    result = jax.random.normal(rng, dims, jnp.float32) * deviation
    if len(shards) > 0:
        result = steps_of(rng, dims, shards, -0.22, 0.18) * result
    return jnp.clip(result, min=-bound, max=bound).astype(kind)


def setup_inputs(seed: int = 0) -> dict:
    key_of = jax.random.split(jax.random.key(seed), 5)
    merged_vectors = bell_draw(key_of[0], (K, N), 1.0, 6.0, ((0, 16), (1, 32)), jnp.float32)
    deflation = draw_deflation(jax.random.fold_in(key_of[4], 71), 0)
    vectors = bell_draw(key_of[2], (BLOCKS, N, NB), (N // 4) ** -0.5, 0.0390625, ((1, 512),), jnp.float32)
    factors = draw_factors(jax.random.fold_in(key_of[4], 71), 0)
    return dict(merged_vectors=merged_vectors, deflation=deflation, vectors=vectors, factors=factors)


contract_plain = (((1,), (0,)), ((), ()))
contract_right = (((1,), (1,)), ((), ()))


def split_parts(values):
    upper = lax.optimization_barrier(values.astype(jnp.bfloat16)).astype(jnp.float32)
    lower = lax.optimization_barrier((values - upper).astype(jnp.bfloat16)).astype(jnp.float32)
    return upper, lower


def exact_dot(first_arg, second_arg, numbers):
    return lax.dot_general(first_arg, second_arg, numbers, precision=lax.Precision.HIGHEST, preferred_element_type=jnp.float32)


def split_dot(first_parts, second_parts, numbers):
    total = exact_dot(first_parts[0], second_parts[0], numbers)
    total = total + exact_dot(first_parts[0], second_parts[1], numbers)
    return total + exact_dot(first_parts[1], second_parts[0], numbers)


def reference(merged_vectors, deflation, vectors, factors):
    current = merged_vectors[deflation]
    for block_id in range(BLOCKS - 1, -1, -1):
        vector_parts = split_parts(vectors[block_id])
        projected = split_dot(split_parts(current), vector_parts, contract_plain)
        combined = exact_dot(projected, factors[block_id], contract_right)
        current = current - split_dot(split_parts(combined), vector_parts, contract_right)
    return current
```

```python
import jax
import jax.numpy as jnp
from jax import lax
from jax.experimental import pallas as pl
from jax.experimental.pallas import tpu as pltpu
from jax.sharding import PartitionSpec as P

MESH = pl.DeviceIdType.MESH
F32, BF16 = jnp.float32, jnp.bfloat16
YN, XN, ZN = 4, 4, 16
NB = 256
BLOCKS = 4
ROWS = 32
SHARD = 200
PAIRS = 3
PLAIN = (((1,), (0,)), ((), ()))
RIGHT = (((1,), (1,)), ((), ()))
LEFT = (((0,), (0,)), ((), ()))


def split_parts(values):
    upper = values.astype(BF16)
    return upper, (values - upper.astype(F32)).astype(BF16)


def dot(a, b, numbers):
    return lax.dot_general(a, b, numbers, preferred_element_type=F32)


def split_dot(a, b, numbers):
    return dot(a[0], b[0], numbers) + dot(a[0], b[1], numbers) + dot(a[1], b[0], numbers)


def device(z, x, y, core):
    return (z * 2 + x // 2, y * 4 + (x % 2) * 2 + core)


def send(src, dst, sems, index, where):
    copy = pltpu.make_async_remote_copy(
        src_ref=src,
        dst_ref=dst,
        send_sem=sems.at[0, index],
        recv_sem=sems.at[1, index],
        device_id=where,
        device_id_type=MESH,
    )
    copy.start()
    return copy


def padded(values):
    return jnp.concatenate([values, jnp.zeros((NB - SHARD, values.shape[1]), F32)], axis=0)


def kernel(
    order_ref, a_ref, v_ref, f_ref, out_ref,
    v_other, v_up, v_low, f_up, f_low,
    a_send, a_recv,
    p_part, p_y, p_x_in, p_x, p_z_in, p_z, p_z_own, p_sum,
    g_part, g_y, g_x_in, g_x, g_z_in, g_z, g_z_own, g_sum, g_all,
    w_all, o_part, o_both, o_send, o_recv,
    v_sems, a_sems, py_sems, px_sems, pz_sems, pg_sems,
    gy_sems, gx_sems, gz_sems, gg_sems, gxa_sems, gya_sems, gc_sems,
    wx_sems, wy_sems, oc_sems, o_sems,
):
    row = lax.axis_index("row")
    col = lax.axis_index("col")
    z, y, core = row // 2, col // 4, col % 2
    x_low = (col // 2) % 2
    x = (row % 2) * 2 + x_low
    chip = y * 2 + x_low
    sent = []

    y_peers = [(d, device(z, x, (y + d) % YN, core)) for d in range(1, YN)]
    x_peers = [(d, device(z, (x + d) % XN, y, core)) for d in range(1, XN)]
    z_peers = [(d, device((z + d) % ZN, x, y, core)) for d in range(1, ZN)]
    group = []
    for dy in range(YN):
        for dx in range(2):
            for dc in range(2):
                group.append(((y + dy) % YN, (x_low + dx) % 2, (core + dc) % 2))
    col_peers = [(row, gy * 4 + gx * 2 + gc) for gy, gx, gc in group[1:]]
    far_x = [device(z, (x // 2 * 2 + 2) % XN + h, y, core) for h in range(2)]
    other_core = (row, y * 4 + x_low * 2 + 1 - core)

    barrier = pltpu.get_barrier_semaphore()
    peers = col_peers + far_x + [peer for _, peer in z_peers]
    for peer in peers:
        pl.semaphore_signal(barrier, inc=1, device_id=peer, device_id_type=MESH)

    a_value = a_ref[...]
    gap = jnp.zeros((ROWS, NB - SHARD), F32)
    for s in range(8):
        first = a_value[:, s * 400 : s * 400 + 200]
        second = a_value[:, s * 400 + 200 : s * 400 + 400]
        a_send[s] = jnp.concatenate([first, gap, second, gap], axis=1)
    a_recv[chip] = a_send[chip]
    for b in range(BLOCKS):
        up, low = split_parts(padded(v_ref[b]))
        v_up[b, core] = up
        v_low[b, core] = low
        up, low = split_parts(f_ref[b])
        f_up[b] = up
        f_low[b] = low

    pl.semaphore_wait(barrier, len(peers))

    v_copy = send(v_ref, v_other, v_sems, 0, other_core)
    sent.append(v_copy)
    a_copies = []
    for i, (gy, gx, gc) in enumerate(group[2::2]):
        a_copies.append(
            send(a_send.at[gy * 2 + gx], a_recv.at[chip], a_sems, i, (row, gy * 4 + gx * 2 + core))
        )
    sent += a_copies

    v_copy.wait_recv()
    for b in range(BLOCKS):
        up, low = split_parts(padded(v_other[b]))
        v_up[b, 1 - core] = up
        v_low[b, 1 - core] = low

    def v_parts(b):
        return v_up[b].reshape(2 * NB, NB), v_low[b].reshape(2 * NB, NB)

    lefts = (3, 3 - core, 2 - core)
    rights = (2 - 2 * core, 1 - core, 1 - core)
    for j in range(PAIRS):
        g_part[j] = split_dot(v_parts(lefts[j]), v_parts(rights[j]), LEFT)

    def start_y(part, into, sems):
        return [
            send(part.at[:, pl.ds((y + d) % YN * 64, 64), :], into.at[d - 1], sems, d - 1, peer)
            for d, peer in y_peers
        ]

    def finish_y(copies, part, into, total):
        for copy in copies:
            copy.wait_recv()
        total[...] = part[:, pl.ds(y * 64, 64), :] + into[0] + into[1] + into[2]

    def start_x(total, into, sems):
        return [
            send(total.at[:, pl.ds((x + d) % XN * 16, 16), :], into.at[d - 1], sems, d - 1, peer)
            for d, peer in x_peers
        ]

    def finish_x(copies, total, into, tiles, count):
        for copy in copies:
            copy.wait_recv()
        value = total[:, pl.ds(x * 16, 16), :] + into[0] + into[1] + into[2]
        for t in range(ZN):
            j, g, h = t // 4, t // 2 % 2, t % 2
            if j < count:
                tiles[t] = value[j, g * 8 : g * 8 + 8, h * 128 : h * 128 + 128]
            else:
                tiles[t] = jnp.zeros((8, 128), F32)

    def start_z(tiles, into, sems):
        return [
            send(tiles.at[(z + d) % ZN], into.at[d - 1], sems, d - 1, peer) for d, peer in z_peers
        ]

    def finish_z(copies, tiles, into, own):
        for copy in copies:
            copy.wait_recv()
        own[z] = tiles[z] + jnp.sum(into[...], axis=0)

    def start_z_back(own, sems):
        return [send(own.at[z], own.at[z], sems, d - 1, peer) for d, peer in z_peers]

    def finish_z_back(copies, own, count):
        for copy in copies:
            copy.wait_recv()
        blocks = []
        for j in range(count):
            halves = [
                jnp.concatenate([own[j * 4 + g * 2], own[j * 4 + g * 2 + 1]], axis=1) for g in range(2)
            ]
            blocks.append(jnp.concatenate(halves, axis=0))
        return blocks

    gy = start_y(g_part, g_y, gy_sems)
    sent += gy

    for copy in a_copies:
        copy.wait_recv()
    a_parts = split_parts(a_recv[...].reshape(8 * ROWS, 2 * NB))
    for b in range(BLOCKS):
        p_part[b] = split_dot(a_parts, v_parts(b), PLAIN)
    py = start_y(p_part, p_y, py_sems)
    sent += py

    finish_y(gy, g_part, g_y, g_x_in)
    gx = start_x(g_x_in, g_x, gx_sems)
    sent += gx
    finish_x(gx, g_x_in, g_x, g_z_in, PAIRS)
    gz = start_z(g_z_in, g_z, gz_sems)
    sent += gz

    finish_y(py, p_part, p_y, p_x_in)
    px = start_x(p_x_in, p_x, px_sems)
    sent += px
    finish_x(px, p_x_in, p_x, p_z_in, BLOCKS)
    pz = start_z(p_z_in, p_z, pz_sems)
    sent += pz

    finish_z(gz, g_z_in, g_z, g_z_own)
    gg = start_z_back(g_z_own, gg_sems)
    sent += gg
    finish_z(pz, p_z_in, p_z, p_z_own)
    pg = start_z_back(p_z_own, pg_sems)
    sent += pg

    for j, block in enumerate(finish_z_back(gg, g_z_own, PAIRS)):
        g_all[core, y, x, j] = block
    mine = g_all.at[core, y, x]
    gxa = [send(mine, mine, gxa_sems, d - 1, peer) for d, peer in x_peers]
    sent += gxa
    for copy in gxa:
        copy.wait_recv()
    mine = g_all.at[core, y]
    gya = [send(mine, mine, gya_sems, d - 1, peer) for d, peer in y_peers]
    sent += gya
    for copy in gya:
        copy.wait_recv()
    mine = g_all.at[core]
    gc = send(mine, mine, gc_sems, 0, other_core)
    sent.append(gc)

    proj = finish_z_back(pg, p_z_own, BLOCKS)
    gc.wait_recv()

    def g_parts(c, j):
        return split_parts(g_all[c, :, :, j].reshape(NB, NB))

    w = {}
    w[3] = split_dot(split_parts(proj[3]), (f_up[3], f_low[3]), RIGHT)
    w3 = split_parts(w[3])
    p2 = proj[2] - split_dot(w3, g_parts(0, 0), PLAIN)
    w[2] = split_dot(split_parts(p2), (f_up[2], f_low[2]), RIGHT)
    w2 = split_parts(w[2])
    p1 = proj[1] - split_dot(w3, g_parts(0, 1), PLAIN) - split_dot(w2, g_parts(0, 2), PLAIN)
    w[1] = split_dot(split_parts(p1), (f_up[1], f_low[1]), RIGHT)
    w1 = split_parts(w[1])
    p0 = (
        proj[0]
        - split_dot(w3, g_parts(1, 0), PLAIN)
        - split_dot(w2, g_parts(1, 1), PLAIN)
        - split_dot(w1, g_parts(1, 2), PLAIN)
    )
    w[0] = split_dot(split_parts(p0), (f_up[0], f_low[0]), RIGHT)
    for b in range(BLOCKS):
        w_all[y, x, b] = w[b]

    mine = w_all.at[y, x]
    wx = [send(mine, mine, wx_sems, d - 1, peer) for d, peer in x_peers]
    sent += wx
    for copy in wx:
        copy.wait_recv()
    mine = w_all.at[y]
    wy = [send(mine, mine, wy_sems, d - 1, peer) for d, peer in y_peers]
    sent += wy
    for copy in wy:
        copy.wait_recv()

    for half in range(2):
        o_part[half] = a_recv[:, :, half * NB : half * NB + NB].reshape(8 * ROWS, NB)
    for b in range(BLOCKS):
        w_parts = split_parts(w_all[:, :, b].reshape(8 * ROWS, NB))
        for half in range(2):
            o_part[half] -= split_dot(w_parts, (v_up[b, half], v_low[b, half]), RIGHT)

    oc = send(o_part.at[1 - core], o_both.at[core], oc_sems, 0, other_core)
    sent.append(oc)
    o_both[core] = o_part[core]
    oc.wait_recv()

    o_copies = []
    for i, (ty, tx, tc) in enumerate(group[1:] + group[:1]):
        target = ty * 4 + tx * 2 + tc

        @pl.loop(0, ROWS, unroll=8)
        def _(k):
            source = order_ref[target * ROWS + k]
            plane = source // ROWS % 2
            place = source // (2 * ROWS) * ROWS + source % ROWS
            o_send[target, pl.ds(k, 1), :] = o_both[plane, pl.ds(place, 1), :]

        if i < 15:
            o_copies.append(send(o_send.at[target], o_recv.at[col], o_sems, i, (row, target)))
    sent += o_copies
    o_recv[col] = o_send[col]
    for copy in o_copies:
        copy.wait_recv()
    for c in range(16):
        out_ref[:, c * SHARD : c * SHARD + SHARD] = o_recv[c][:, :SHARD]

    for copy in sent:
        copy.wait_send()


def vmem(*shape):
    return pltpu.VMEM(shape, F32)


def half_vmem(*shape):
    return pltpu.VMEM(shape, BF16)


def sems(count):
    return pltpu.SemaphoreType.DMA((2, count))


def per_device(merged_vectors, deflation, vectors, factors):
    rows = 8 * ROWS
    reduce_bufs = lambda n: [
        vmem(n, rows, NB), vmem(YN - 1, n, 64, NB), vmem(n, 64, NB), vmem(XN - 1, n, 16, NB),
        vmem(ZN, 8, 128), vmem(ZN - 1, 8, 128), vmem(ZN, 8, 128), vmem(n, 16, NB),
    ]
    scratch = [
        vmem(BLOCKS, SHARD, NB),
        half_vmem(BLOCKS, 2, NB, NB), half_vmem(BLOCKS, 2, NB, NB),
        half_vmem(BLOCKS, NB, NB), half_vmem(BLOCKS, NB, NB),
        vmem(8, ROWS, 2 * NB), vmem(8, ROWS, 2 * NB),
        *reduce_bufs(BLOCKS),
        *reduce_bufs(PAIRS),
        vmem(2, YN, XN, PAIRS, 16, NB),
        vmem(YN, XN, BLOCKS, 16, NB),
        vmem(2, rows, NB), vmem(2, rows, NB),
        vmem(16, ROWS, NB), vmem(16, ROWS, NB),
        sems(1), sems(7), sems(3), sems(3), sems(15), sems(15),
        sems(3), sems(3), sems(15), sems(15), sems(3), sems(3), sems(1),
        sems(3), sems(3), sems(1), sems(15),
    ]
    in_vmem = pl.BlockSpec(memory_space=pltpu.VMEM)
    return pl.pallas_call(
        kernel,
        out_shape=jax.ShapeDtypeStruct(merged_vectors.shape, F32),
        in_specs=[pl.BlockSpec(memory_space=pltpu.SMEM), in_vmem, in_vmem, in_vmem],
        out_specs=in_vmem,
        scratch_shapes=scratch,
        compiler_params=pltpu.CompilerParams(
            collective_id=0, has_side_effects=True, vmem_limit_bytes=48 * 1024 * 1024
        ),
        name="back_transform",
    )(deflation, merged_vectors, vectors, factors)


def solution(mesh):
    in_specs = (P("col", "row"), P(), P(None, ("row", "col"), None), P())
    out_specs = P("col", "row")
    return jax.shard_map(
        per_device, mesh=mesh, in_specs=in_specs, out_specs=out_specs, check_vma=False
    )
```

```python
import jax
import jax.numpy as jnp
from jax import lax
from jax.experimental import pallas as pl
from jax.experimental.pallas import tpu as pltpu
from jax.sharding import PartitionSpec as P

MESH = pl.DeviceIdType.MESH
F32, BF16 = jnp.float32, jnp.bfloat16
YN, XN, ZN = 4, 4, 16
NB = 256
BLOCKS = 4
ROWS = 32
SHARD = 200
PAIRS = 3
PLAIN = (((1,), (0,)), ((), ()))
RIGHT = (((1,), (1,)), ((), ()))
LEFT = (((0,), (0,)), ((), ()))


def split_parts(values):
    upper = values.astype(BF16)
    return upper, (values - upper.astype(F32)).astype(BF16)


def dot(a, b, numbers):
    return lax.dot_general(a, b, numbers, preferred_element_type=F32)


def split_dot(a, b, numbers):
    return dot(a[0], b[0], numbers) + dot(a[0], b[1], numbers) + dot(a[1], b[0], numbers)


def device(z, x, y, core):
    return (z * 2 + x // 2, y * 4 + (x % 2) * 2 + core)


def send(src, dst, sems, index, where):
    copy = pltpu.make_async_remote_copy(
        src_ref=src,
        dst_ref=dst,
        send_sem=sems.at[0, index],
        recv_sem=sems.at[1, index],
        device_id=where,
        device_id_type=MESH,
    )
    copy.start()
    return copy


def padded(values):
    return jnp.concatenate([values, jnp.zeros((NB - SHARD, values.shape[1]), F32)], axis=0)


def kernel(
    order_hbm, a_hbm, v_hbm, f_hbm, out_ref,
    order_ref, a_ref, v_ref, f_ref,
    v_other, v_up, v_low, f_up, f_low,
    a_send, a_recv,
    p_part, p_in1, p_mid, p_in2, p_tiles, p_in3, p_own,
    g_part, g_in1, g_mid, g_in2, g_tiles, g_in3, g_own,
    g_all, w_all, o_part, o_both, o_send, o_recv,
    in_sems, v_sems, a_sems, p1_sems, p2_sems, p3_sems, p4_sems,
    g1_sems, g2_sems, g3_sems, g4_sems, g5_sems, g6_sems, g7_sems,
    w1_sems, w2_sems, oc_sems, o_sems,
):
    row = lax.axis_index("row")
    col = lax.axis_index("col")
    z, y, core = row // 2, col // 4, col % 2
    x_low = (col // 2) % 2
    x = (row % 2) * 2 + x_low
    chip = y * 2 + x_low
    sent = []

    y_peers = [(d, (y + d) % YN, device(z, x, (y + d) % YN, core)) for d in (2, 1, 3)]
    x_peers = [(d, (x + d) % XN, device(z, (x + d) % XN, y, core)) for d in (2, 1, 3)]
    far_first = sorted(range(1, ZN), key=lambda d: -min(d, ZN - d))
    z_peers = [(d, (z + d) % ZN, device((z + d) % ZN, x, y, core)) for d in far_first]
    group = []
    for dy in (2, 1, 3, 0):
        for dx in (1, 0):
            for dc in (1, 0):
                group.append(((y + dy) % YN, (x_low + dx) % 2, (core + dc) % 2))
    col_peers = [(row, gy * 4 + gx * 2 + gc) for gy, gx, gc in group[:-1]]
    far_x = [device(z, (x // 2 * 2 + 2) % XN + h, y, core) for h in range(2)]
    other_core = (row, y * 4 + x_low * 2 + 1 - core)

    barrier = pltpu.get_barrier_semaphore()
    peers = col_peers + far_x + [peer for _, _, peer in z_peers]
    for peer in peers:
        pl.semaphore_signal(barrier, inc=1, device_id=peer, device_id_type=MESH)

    inputs = [
        pltpu.make_async_copy(src, dst, in_sems.at[i])
        for i, (src, dst) in enumerate(
            ((a_hbm, a_ref), (v_hbm, v_ref), (f_hbm, f_ref), (order_hbm, order_ref))
        )
    ]
    for copy in inputs:
        copy.start()

    inputs[0].wait()
    a_value = a_ref[...]
    gap = jnp.zeros((ROWS, NB - SHARD), F32)
    for s in range(8):
        first = a_value[:, s * 400 : s * 400 + 200]
        second = a_value[:, s * 400 + 200 : s * 400 + 400]
        a_send[s] = jnp.concatenate([first, gap, second, gap], axis=1)
    a_recv[chip] = a_send[chip]
    inputs[1].wait()
    for b in range(BLOCKS):
        up, low = split_parts(padded(v_ref[b]))
        v_up[b, core] = up
        v_low[b, core] = low
    inputs[2].wait()
    for b in range(BLOCKS):
        up, low = split_parts(f_ref[b])
        f_up[b] = up
        f_low[b] = low
    inputs[3].wait()

    pl.semaphore_wait(barrier, len(peers))
    v_copy = send(v_ref, v_other, v_sems, 0, other_core)
    sent.append(v_copy)
    a_copies = []
    for i, (gy, gx, gc) in enumerate(group[1:-1:2]):
        a_copies.append(
            send(a_send.at[gy * 2 + gx], a_recv.at[chip], a_sems, i, (row, gy * 4 + gx * 2 + core))
        )
    sent += a_copies

    v_copy.wait_recv()
    for b in range(BLOCKS):
        up, low = split_parts(padded(v_other[b]))
        v_up[b, 1 - core] = up
        v_low[b, 1 - core] = low

    def v_parts(b):
        return v_up[b].reshape(2 * NB, NB), v_low[b].reshape(2 * NB, NB)

    def start_first(half, part, into, sems):
        copies = []
        for d, place, peer in (y_peers, x_peers)[half]:
            src = part.at[0, :, place] if half == 0 else part.at[1, :, :, place]
            copies.append(send(src, into.at[half, d - 1], sems, half * 3 + d - 1, peer))
        sent.extend(copies)
        return copies

    def finish_first(half, copies, part, into, mid):
        for copy in copies:
            copy.wait_recv()
        own = part[0, :, y] if half == 0 else part[1, :, :, x]
        mid[half] = own + into[half, 0] + into[half, 1] + into[half, 2]

    def start_second(half, mid, into, sems):
        copies = []
        for d, place, peer in (x_peers, y_peers)[half]:
            src = mid.at[half, :, place]
            copies.append(send(src, into.at[half, d - 1], sems, half * 3 + d - 1, peer))
        sent.extend(copies)
        return copies

    def finish_second(half, copies, mid, into, tiles):
        for copy in copies:
            copy.wait_recv()
        value = mid[half, :, (x, y)[half]] + into[half, 0] + into[half, 1] + into[half, 2]
        count, lanes = value.shape[0], value.shape[2] // 128
        for t in range(count * 2 * lanes):
            j, g, h = t // (2 * lanes), t // lanes % 2, t % lanes
            piece = value[j, g * 8 : g * 8 + 8, h * 128 : h * 128 + 128]
            tiles[half * count * 2 * lanes + t] = piece

    def start_z(tiles, into, sems):
        copies = [
            send(tiles.at[place], into.at[d - 1], sems, d - 1, peer) for d, place, peer in z_peers
        ]
        sent.extend(copies)
        return copies

    def finish_z(copies, tiles, into, own):
        for copy in copies:
            copy.wait_recv()
        own[z] = tiles[z] + jnp.sum(into[...], axis=0)

    def start_z_back(own, sems):
        copies = [send(own.at[z], own.at[z], sems, d - 1, peer) for d, _, peer in z_peers]
        sent.extend(copies)
        return copies

    def finish_z_back(copies, own, count, lanes):
        for copy in copies:
            copy.wait_recv()
        blocks = []
        for j in range(2 * count):
            base = j * 2 * lanes
            halves = [
                jnp.concatenate([own[base + g * lanes + h] for h in range(lanes)], axis=1)
                for g in range(2)
            ]
            blocks.append(jnp.concatenate(halves, axis=0))
        return blocks

    def start_back(half, whole, sems):
        mine = whole.at[half, :, y, x]
        copies = [
            send(mine, mine, sems, half * 3 + d - 1, peer) for d, _, peer in (x_peers, y_peers)[half]
        ]
        sent.extend(copies)
        return copies

    def finish_back(half, whole, copies, sems):
        for copy in copies:
            copy.wait_recv()
        mine = whole.at[0, :, y] if half == 0 else whole.at[1, :, :, x]
        copies = [
            send(mine, mine, sems, half * 3 + d - 1, peer) for d, _, peer in (y_peers, x_peers)[half]
        ]
        sent.extend(copies)
        return copies

    lefts = (3, 3 - core, 2 - core)
    rights = (2 - 2 * core, 1 - core, 1 - core)
    for j in range(PAIRS):
        product = split_dot(v_parts(lefts[j]), v_parts(rights[j]), LEFT)
        for half in range(2):
            lanes = product[:, half * 128 : half * 128 + 128]
            g_part[half, j] = lanes.reshape(YN, XN, 16, 128)
    g1 = [start_first(half, g_part, g_in1, g1_sems) for half in range(2)]

    for copy in a_copies:
        copy.wait_recv()
    a_parts = split_parts(a_recv[...].reshape(8 * ROWS, 2 * NB))
    p1 = []
    for half in range(2):
        for i in range(2):
            product = split_dot(a_parts, v_parts(3 - 2 * half - i), PLAIN)
            p_part[half, i] = product.reshape(YN, XN, 16, NB)
        p1.append(start_first(half, p_part, p_in1, p1_sems))

    g2 = []
    for half in range(2):
        finish_first(half, g1[half], g_part, g_in1, g_mid)
        g2.append(start_second(half, g_mid, g_in2, g2_sems))
    for half in range(2):
        finish_second(half, g2[half], g_mid, g_in2, g_tiles)
    for t in range(12, ZN):
        g_tiles[t] = jnp.zeros((8, 128), F32)
    g3 = start_z(g_tiles, g_in3, g3_sems)

    p2 = []
    for half in range(2):
        finish_first(half, p1[half], p_part, p_in1, p_mid)
        p2.append(start_second(half, p_mid, p_in2, p2_sems))
    for half in range(2):
        finish_second(half, p2[half], p_mid, p_in2, p_tiles)
    p3 = start_z(p_tiles, p_in3, p3_sems)

    finish_z(g3, g_tiles, g_in3, g_own)
    g4 = start_z_back(g_own, g4_sems)
    finish_z(p3, p_tiles, p_in3, p_own)
    p4 = start_z_back(p_own, p4_sems)

    g_mine = g_all.at[core]
    for j, block in enumerate(finish_z_back(g4, g_own, PAIRS, 1)):
        g_all[core, j // PAIRS, j % PAIRS, y, x] = block
    g5 = [start_back(half, g_mine, g5_sems) for half in range(2)]
    g6 = [finish_back(half, g_mine, g5[half], g6_sems) for half in range(2)]
    g7 = []
    for half in range(2):
        where = y if half == 0 else x
        arrived = [(where, None)] + [
            ((where - d) % 4, copy) for d, copy in zip((2, 1, 3), g6[half])
        ]
        for i, (place, copy) in enumerate(arrived):
            if copy is not None:
                copy.wait_recv()
            piece = g_mine.at[0, :, place] if half == 0 else g_mine.at[1, :, :, place]
            g7.append(send(piece, piece, g7_sems, half * 4 + i, other_core))
    sent += g7

    proj = finish_z_back(p4, p_own, 2, 2)
    w = [None] * BLOCKS
    w[0] = split_dot(split_parts(proj[0]), (f_up[3], f_low[3]), RIGHT)
    for copy in g7:
        copy.wait_recv()

    def g_parts(c, j):
        block = jnp.concatenate(
            [g_all[c, half, j].reshape(NB, 128) for half in range(2)], axis=1
        )
        return split_parts(block)

    places = {(0, 1): (0, 0), (0, 2): (0, 1), (1, 2): (0, 2), (0, 3): (1, 0), (1, 3): (1, 1), (2, 3): (1, 2)}
    w_parts = [split_parts(w[0])]
    w_all[0, 0, y, x] = w[0]
    w1 = []
    for i in range(1, BLOCKS):
        value = proj[i]
        for k in range(i):
            value = value - split_dot(w_parts[k], g_parts(*places[k, i]), PLAIN)
        value = split_dot(split_parts(value), (f_up[3 - i], f_low[3 - i]), RIGHT)
        w_parts.append(split_parts(value))
        w_all[i // 2, i % 2, y, x] = value
        if i % 2 == 1:
            w1.append(start_back(i // 2, w_all, w1_sems))
    w2 = [finish_back(half, w_all, w1[half], w2_sems) for half in range(2)]

    for side in range(2):
        o_part[side] = a_recv[:, :, side * NB : side * NB + NB].reshape(8 * ROWS, NB)
    for half in range(2):
        for copy in w2[half]:
            copy.wait_recv()
        for i in range(2):
            b = 3 - 2 * half - i
            parts = split_parts(w_all[half, i].reshape(8 * ROWS, NB))
            for side in range(2):
                o_part[side] -= split_dot(parts, (v_up[b, side], v_low[b, side]), RIGHT)
    oc = send(o_part.at[1 - core], o_both.at[core], oc_sems, 0, other_core)
    sent.append(oc)
    o_both[core] = o_part[core]
    oc.wait_recv()
    o_copies = []
    for i, (ty, tx, tc) in enumerate(group):
        target = ty * 4 + tx * 2 + tc

        @pl.loop(0, ROWS, unroll=8)
        def _(k):
            source = order_ref[target * ROWS + k]
            plane = source // ROWS % 2
            place = source // (2 * ROWS) * ROWS + source % ROWS
            o_send[target, pl.ds(k, 1), :] = o_both[plane, pl.ds(place, 1), :]

        if i < 15:
            o_copies.append(send(o_send.at[target], o_recv.at[col], o_sems, i, (row, target)))
    sent += o_copies
    o_recv[col] = o_send[col]
    for copy in o_copies:
        copy.wait_recv()
    for c in range(16):
        out_ref[:, c * SHARD : c * SHARD + SHARD] = o_recv[c][:, :SHARD]

    for copy in sent:
        copy.wait_send()


def vmem(*shape):
    return pltpu.VMEM(shape, F32)


def half_vmem(*shape):
    return pltpu.VMEM(shape, BF16)


def sems(count):
    return pltpu.SemaphoreType.DMA((2, count))


def reduce_bufs(n, lanes):
    return [
        vmem(2, n, YN, XN, 16, lanes), vmem(2, 3, n, 4, 16, lanes), vmem(2, n, 4, 16, lanes),
        vmem(2, 3, n, 16, lanes), vmem(ZN, 8, 128), vmem(ZN - 1, 8, 128), vmem(ZN, 8, 128),
    ]


def per_device(merged_vectors, deflation, vectors, factors):
    rows = 8 * ROWS
    scratch = [
        pltpu.SMEM(deflation.shape, jnp.int32), vmem(*merged_vectors.shape),
        vmem(*vectors.shape), vmem(*factors.shape),
        vmem(BLOCKS, SHARD, NB),
        half_vmem(BLOCKS, 2, NB, NB), half_vmem(BLOCKS, 2, NB, NB),
        half_vmem(BLOCKS, NB, NB), half_vmem(BLOCKS, NB, NB),
        vmem(8, ROWS, 2 * NB), vmem(8, ROWS, 2 * NB),
        *reduce_bufs(2, NB),
        *reduce_bufs(PAIRS, 128),
        vmem(2, 2, PAIRS, YN, XN, 16, 128),
        vmem(2, 2, YN, XN, 16, NB),
        vmem(2, rows, NB), vmem(2, rows, NB),
        vmem(16, ROWS, NB), vmem(16, ROWS, NB),
        pltpu.SemaphoreType.DMA((4,)),
        sems(1), sems(7), sems(6), sems(6), sems(15), sems(15),
        sems(6), sems(6), sems(15), sems(15), sems(6), sems(6), sems(8),
        sems(6), sems(6), sems(1), sems(15),
    ]
    in_place = pl.BlockSpec(memory_space=pl.ANY)
    return pl.pallas_call(
        kernel,
        out_shape=jax.ShapeDtypeStruct(merged_vectors.shape, F32),
        in_specs=[in_place] * 4,
        out_specs=pl.BlockSpec(memory_space=pltpu.VMEM),
        scratch_shapes=scratch,
        compiler_params=pltpu.CompilerParams(
            collective_id=0, has_side_effects=True, vmem_limit_bytes=56 * 1024 * 1024
        ),
        name="back_transform",
    )(deflation, merged_vectors, vectors, factors)


def solution(mesh):
    in_specs = (P("col", "row"), P(), P(None, ("row", "col"), None), P())
    out_specs = P("col", "row")
    return jax.shard_map(
        per_device, mesh=mesh, in_specs=in_specs, out_specs=out_specs, check_vma=False
    )
```

```python
import jax
import jax.numpy as jnp
from jax import lax
from jax.experimental import pallas as pl
from jax.experimental.pallas import tpu as pltpu
from jax.sharding import PartitionSpec as P

MESH = pl.DeviceIdType.MESH
F32, BF16 = jnp.float32, jnp.bfloat16
YN, XN, ZN = 4, 4, 16
NB = 256
BLOCKS = 4
ROWS = 32
SHARD = 200
HALF = 128
PAIRS = 3
PLAIN = (((1,), (0,)), ((), ()))
RIGHT = (((1,), (1,)), ((), ()))
LEFT = (((0,), (0,)), ((), ()))


def split_parts(values):
    upper = values.astype(BF16)
    return upper, (values - upper.astype(F32)).astype(BF16)


def dot(a, b, numbers):
    return lax.dot_general(a, b, numbers, preferred_element_type=F32)


def split_dot(a, b, numbers):
    return dot(a[0], b[0], numbers) + dot(a[0], b[1], numbers) + dot(a[1], b[0], numbers)


def device(z, x, y, core):
    return (z * 2 + x // 2, y * 4 + (x % 2) * 2 + core)


def send(src, dst, sems, index, where):
    copy = pltpu.make_async_remote_copy(
        src_ref=src,
        dst_ref=dst,
        send_sem=sems.at[0, index],
        recv_sem=sems.at[1, index],
        device_id=where,
        device_id_type=MESH,
    )
    copy.start()
    return copy


def padded(values):
    rows = jnp.concatenate([values, jnp.zeros((NB - SHARD, values.shape[1]), F32)], axis=0)
    return rows.reshape(2, HALF, values.shape[1])


def kernel(
    order_hbm, a_hbm, v_hbm, f_hbm, out_ref,
    order_ref, place_ref, a_ref, v_ref, f_ref,
    v_other, v_up, v_low, f_up, f_low,
    a_send, a_recv,
    p_part, p_in1, p_mid, p_in2, p_tiles, p_in3, p_own,
    g_part, g_in1, g_mid, g_in2, g_tiles, g_in3, g_own,
    g_own_part, g_all, w_all, o_part, o_sides, o_both0, o_both1, o_send, o_recv,
    in_sems, v_sems, a_sems, p1_sems, p2_sems, p3_sems, p4_sems,
    g1_sems, g2_sems, g3_sems, g4_sems, g5_sems, g6_sems, g7_sems,
    w1_sems, w2_sems, oc_sems, o_sems, known_sems,
):
    row = lax.axis_index("row")
    col = lax.axis_index("col")
    z, y, core = row // 2, col // 4, col % 2
    x_low = (col // 2) % 2
    x = (row % 2) * 2 + x_low
    chip = y * 2 + x_low
    sent = []

    y_peers = [(d, (y + d) % YN, device(z, x, (y + d) % YN, core)) for d in (2, 1, 3)]
    x_peers = [(d, (x + d) % XN, device(z, (x + d) % XN, y, core)) for d in (2, 1, 3)]
    far_first = sorted(range(1, ZN), key=lambda d: -min(d, ZN - d))
    z_peers = [(d, (z + d) % ZN, device((z + d) % ZN, x, y, core)) for d in far_first]
    group = []
    for dy in (2, 1, 3, 0):
        for dx in (1, 0):
            for dc in (1, 0):
                group.append(((y + dy) % YN, (x_low + dx) % 2, (core + dc) % 2))
    col_peers = [(row, gy * 4 + gx * 2 + gc) for gy, gx, gc in group[:-1]]
    far_x = [device(z, (x // 2 * 2 + 2) % XN + h, y, core) for h in range(2)]
    other_core = (row, y * 4 + x_low * 2 + 1 - core)

    barrier = pltpu.get_barrier_semaphore()
    near_z = [device((z + d) % ZN, x, y, core) for d in (1, ZN - 1)]
    peers = col_peers + far_x + near_z
    for peer in peers:
        pl.semaphore_signal(barrier, inc=1, device_id=peer, device_id_type=MESH)

    def tell(step):
        for d in (1 << step, ZN - (1 << step)):
            where = device((z + d) % ZN, x, y, core)
            pl.semaphore_signal(known_sems.at[step], inc=1, device_id=where, device_id_type=MESH)

    def hear(step):
        pl.semaphore_wait(known_sems.at[step], 2)

    inputs = [
        pltpu.make_async_copy(src, dst, in_sems.at[i])
        for i, (src, dst) in enumerate(
            ((v_hbm, v_ref), (a_hbm, a_ref), (f_hbm, f_ref), (order_hbm, order_ref))
        )
    ]
    for copy in inputs:
        copy.start()

    inputs[0].wait()
    pl.semaphore_wait(barrier, len(peers))
    tell(0)
    v_copy = send(v_ref, v_other, v_sems, 0, other_core)
    sent.append(v_copy)
    inputs[1].wait()
    a_value = a_ref[...]
    gap = jnp.zeros((ROWS, NB - SHARD), F32)
    for s in range(8):
        first, second = s * 2 * SHARD, (s * 2 + 1) * SHARD
        pieces = [
            a_value[:, first : first + HALF],
            a_value[:, second : second + HALF],
            a_value[:, first + HALF : first + SHARD],
            gap,
            a_value[:, second + HALF : second + SHARD],
            gap,
        ]
        a_send[s] = jnp.concatenate(pieces, axis=1)
    a_recv[chip] = a_send[chip]
    a_copies = []
    for i, (gy, gx, gc) in enumerate(group[1:-1:2]):
        a_copies.append(
            send(a_send.at[gy * 2 + gx], a_recv.at[chip], a_sems, i, (row, gy * 4 + gx * 2 + core))
        )
    sent += a_copies

    for b in range(BLOCKS):
        up, low = split_parts(padded(v_ref[b]))
        v_up[b, :, core] = up
        v_low[b, :, core] = low

    def own_parts(b):
        return v_up[b, :, core].reshape(NB, NB), v_low[b, :, core].reshape(NB, NB)

    lefts = (3, 3 - core, 2 - core)
    rights = (2 - 2 * core, 1 - core, 1 - core)
    for j in range(PAIRS):
        g_own_part[j] = split_dot(own_parts(lefts[j]), own_parts(rights[j]), LEFT)

    hear(0)
    tell(1)
    v_copy.wait_recv()
    for b in range(BLOCKS):
        up, low = split_parts(padded(v_other[b]))
        v_up[b, :, 1 - core] = up
        v_low[b, :, 1 - core] = low

    def other_parts(b):
        return v_up[b, :, 1 - core].reshape(NB, NB), v_low[b, :, 1 - core].reshape(NB, NB)

    def v_parts(b):
        return v_up[b].reshape(2 * NB, NB), v_low[b].reshape(2 * NB, NB)

    def start_first(half, part, into, sems):
        copies = []
        for d, place, peer in (y_peers, x_peers)[half]:
            src = part.at[0, :, place] if half == 0 else part.at[1, :, :, place]
            copies.append(send(src, into.at[half, d - 1], sems, half * 3 + d - 1, peer))
        sent.extend(copies)
        return copies

    def finish_first(half, copies, part, into, mid):
        for copy in copies:
            copy.wait_recv()
        own = part[0, :, y] if half == 0 else part[1, :, :, x]
        mid[half] = own + into[half, 0] + into[half, 1] + into[half, 2]

    def start_second(half, mid, into, sems):
        copies = []
        for d, place, peer in (x_peers, y_peers)[half]:
            src = mid.at[half, :, place]
            copies.append(send(src, into.at[half, d - 1], sems, half * 3 + d - 1, peer))
        sent.extend(copies)
        return copies

    def finish_second(half, copies, mid, into, tiles):
        for copy in copies:
            copy.wait_recv()
        value = mid[half, :, (x, y)[half]] + into[half, 0] + into[half, 1] + into[half, 2]
        count, lanes = value.shape[0], value.shape[2] // 128
        for t in range(count * 2 * lanes):
            j, g, h = t // (2 * lanes), t // lanes % 2, t % lanes
            piece = value[j, g * 8 : g * 8 + 8, h * 128 : h * 128 + 128]
            tiles[half * count * 2 * lanes + t] = piece

    def start_z(tiles, into, sems):
        copies = [
            send(tiles.at[place], into.at[d - 1], sems, d - 1, peer) for d, place, peer in z_peers
        ]
        sent.extend(copies)
        return copies

    def finish_z(copies, tiles, into, own):
        for copy in copies:
            copy.wait_recv()
        own[z] = tiles[z] + jnp.sum(into[...], axis=0)

    def start_z_back(own, sems):
        copies = [send(own.at[z], own.at[z], sems, d - 1, peer) for d, _, peer in z_peers]
        sent.extend(copies)
        return copies

    def finish_z_back(copies, own, count, lanes):
        for copy in copies:
            copy.wait_recv()
        blocks = []
        for j in range(2 * count):
            base = j * 2 * lanes
            halves = [
                jnp.concatenate([own[base + g * lanes + h] for h in range(lanes)], axis=1)
                for g in range(2)
            ]
            blocks.append(jnp.concatenate(halves, axis=0))
        return blocks

    def start_back(half, whole, sems):
        mine = whole.at[half, :, y, x]
        copies = [
            send(mine, mine, sems, half * 3 + d - 1, peer) for d, _, peer in (x_peers, y_peers)[half]
        ]
        sent.extend(copies)
        return copies

    def finish_back(half, whole, copies, sems):
        for copy in copies:
            copy.wait_recv()
        mine = whole.at[0, :, y] if half == 0 else whole.at[1, :, :, x]
        copies = [
            send(mine, mine, sems, half * 3 + d - 1, peer) for d, _, peer in (y_peers, x_peers)[half]
        ]
        sent.extend(copies)
        return copies

    for j in range(PAIRS):
        product = g_own_part[j] + split_dot(other_parts(lefts[j]), other_parts(rights[j]), LEFT)
        for half in range(2):
            lanes = product[:, half * 128 : half * 128 + 128]
            g_part[half, j] = lanes.reshape(YN, XN, 16, 128)
    g1 = [start_first(half, g_part, g_in1, g1_sems) for half in range(2)]
    hear(1)
    tell(2)

    g2 = []
    for half in range(2):
        finish_first(half, g1[half], g_part, g_in1, g_mid)
        g2.append(start_second(half, g_mid, g_in2, g2_sems))

    for copy in a_copies:
        copy.wait_recv()
    a_parts = split_parts(a_recv[...].reshape(8 * ROWS, 2 * NB))
    p1 = []
    for half in range(2):
        for i in range(2):
            product = split_dot(a_parts, v_parts(3 - 2 * half - i), PLAIN)
            p_part[half, i] = product.reshape(YN, XN, 16, NB)
        p1.append(start_first(half, p_part, p_in1, p1_sems))

    for half in range(2):
        finish_second(half, g2[half], g_mid, g_in2, g_tiles)
    for t in range(12, ZN):
        g_tiles[t] = jnp.zeros((8, 128), F32)
    hear(2)
    g3 = start_z(g_tiles, g_in3, g3_sems)

    inputs[2].wait()
    for b in range(BLOCKS):
        up, low = split_parts(f_ref[b])
        f_up[b] = up
        f_low[b] = low
    inputs[3].wait()

    @pl.loop(0, 16 * ROWS, unroll=8)
    def _(k):
        source = order_ref[k]
        place_ref[k] = (source >> 5 & 1) * (8 * ROWS) + (source >> 6) * ROWS + (source & 31)

    p2 = []
    for half in range(2):
        finish_first(half, p1[half], p_part, p_in1, p_mid)
        p2.append(start_second(half, p_mid, p_in2, p2_sems))
    finish_z(g3, g_tiles, g_in3, g_own)
    g4 = start_z_back(g_own, g4_sems)
    for half in range(2):
        finish_second(half, p2[half], p_mid, p_in2, p_tiles)
    p3 = start_z(p_tiles, p_in3, p3_sems)

    g_mine = g_all.at[core]
    for j, block in enumerate(finish_z_back(g4, g_own, PAIRS, 1)):
        g_all[core, j // PAIRS, j % PAIRS, y, x] = block
    g5 = [start_back(half, g_mine, g5_sems) for half in range(2)]
    finish_z(p3, p_tiles, p_in3, p_own)
    p4 = start_z_back(p_own, p4_sems)
    g6 = [finish_back(half, g_mine, g5[half], g6_sems) for half in range(2)]
    g7 = []
    for half in range(2):
        where = y if half == 0 else x
        arrived = [(where, None)] + [
            ((where - d) % 4, copy) for d, copy in zip((2, 1, 3), g6[half])
        ]
        for i, (place, copy) in enumerate(arrived):
            if copy is not None:
                copy.wait_recv()
            piece = g_mine.at[0, :, place] if half == 0 else g_mine.at[1, :, :, place]
            g7.append(send(piece, piece, g7_sems, half * 4 + i, other_core))
    sent += g7

    proj = finish_z_back(p4, p_own, 2, 2)
    w = [None] * BLOCKS
    w[0] = split_dot(split_parts(proj[0]), (f_up[3], f_low[3]), RIGHT)
    for copy in g7:
        copy.wait_recv()

    def g_parts(c, j):
        block = jnp.concatenate(
            [g_all[c, half, j].reshape(NB, 128) for half in range(2)], axis=1
        )
        return split_parts(block)

    places = {(0, 1): (0, 0), (0, 2): (0, 1), (1, 2): (0, 2), (0, 3): (1, 0), (1, 3): (1, 1), (2, 3): (1, 2)}
    w_parts = [split_parts(w[0])]
    w_all[0, 0, y, x] = w[0]
    w1 = []
    for i in range(1, BLOCKS):
        value = proj[i]
        for k in range(i):
            value = value - split_dot(w_parts[k], g_parts(*places[k, i]), PLAIN)
        value = split_dot(split_parts(value), (f_up[3 - i], f_low[3 - i]), RIGHT)
        w_parts.append(split_parts(value))
        w_all[i // 2, i % 2, y, x] = value
        if i % 2 == 1:
            w1.append(start_back(i // 2, w_all, w1_sems))
    w2 = [finish_back(half, w_all, w1[half], w2_sems) for half in range(2)]

    w_blocks = {}
    o_both = (o_both0, o_both1)
    for part in range(2):
        o_part[part] = a_recv[:, :, part * NB : part * NB + NB].reshape(8 * ROWS, NB)
    oc = []
    for half in range(2):
        for copy in w2[half]:
            copy.wait_recv()
        for i in range(2):
            w_blocks[half, i] = split_parts(w_all[half, i].reshape(8 * ROWS, NB))
        for part in range(2):
            value = o_part[part]
            for i in range(2):
                b = 3 - 2 * half - i
                v_block = (v_up[b, part].reshape(NB, NB), v_low[b, part].reshape(NB, NB))
                value = value - split_dot(w_blocks[half, i], v_block, RIGHT)
            if half == 0:
                o_part[part] = value
            else:
                for side in range(2):
                    o_sides[part, side] = value[:, side * HALF : side * HALF + HALF]
                into = o_both[part].at[pl.ds(core * 8 * ROWS, 8 * ROWS)]
                oc.append(send(o_sides.at[part, 1 - core], into, oc_sems, part, other_core))
                o_both[part][pl.ds(core * 8 * ROWS, 8 * ROWS)] = o_sides[part, core]
    sent += oc
    o_copies = []
    for part in range(2):
        oc[part].wait_recv()
        for i, (ty, tx, tc) in enumerate(group):
            target = ty * 4 + tx * 2 + tc

            @pl.loop(0, ROWS, unroll=16)
            def _(k):
                place = place_ref[target * ROWS + k]
                o_send[part, target, pl.ds(k, 1), :] = o_both[part][pl.ds(place, 1), :]

            if i < 15:
                src, dst = o_send.at[part, target], o_recv.at[part, col]
                o_copies.append(send(src, dst, o_sems, part * 15 + i, (row, target)))
    sent += o_copies
    for part in range(2):
        o_recv[part, col] = o_send[part, col]
    for copy in o_copies:
        copy.wait_recv()
    for c in range(16):
        out_ref[:, c * SHARD : c * SHARD + HALF] = o_recv[0, c]
        out_ref[:, c * SHARD + HALF : c * SHARD + SHARD] = o_recv[1, c][:, : SHARD - HALF]

    for copy in sent:
        copy.wait_send()


def vmem(*shape):
    return pltpu.VMEM(shape, F32)


def half_vmem(*shape):
    return pltpu.VMEM(shape, BF16)


def sems(count):
    return pltpu.SemaphoreType.DMA((2, count))


def reduce_bufs(n, lanes):
    return [
        vmem(2, n, YN, XN, 16, lanes), vmem(2, 3, n, 4, 16, lanes), vmem(2, n, 4, 16, lanes),
        vmem(2, 3, n, 16, lanes), vmem(ZN, 8, 128), vmem(ZN - 1, 8, 128), vmem(ZN, 8, 128),
    ]


def per_device(merged_vectors, deflation, vectors, factors):
    rows = 8 * ROWS
    scratch = [
        pltpu.SMEM(deflation.shape, jnp.int32), pltpu.SMEM(deflation.shape, jnp.int32),
        vmem(*merged_vectors.shape),
        vmem(*vectors.shape), vmem(*factors.shape),
        vmem(BLOCKS, SHARD, NB),
        half_vmem(BLOCKS, 2, 2, HALF, NB), half_vmem(BLOCKS, 2, 2, HALF, NB),
        half_vmem(BLOCKS, NB, NB), half_vmem(BLOCKS, NB, NB),
        vmem(8, ROWS, 2 * NB), vmem(8, ROWS, 2 * NB),
        *reduce_bufs(2, NB),
        *reduce_bufs(PAIRS, 128),
        vmem(PAIRS, NB, NB),
        vmem(2, 2, PAIRS, YN, XN, 16, 128),
        vmem(2, 2, YN, XN, 16, NB),
        vmem(2, rows, NB), vmem(2, 2, rows, HALF), vmem(2 * rows, HALF), vmem(2 * rows, HALF),
        vmem(2, 16, ROWS, HALF), vmem(2, 16, ROWS, HALF),
        pltpu.SemaphoreType.DMA((4,)),
        sems(1), sems(7), sems(6), sems(6), sems(15), sems(15),
        sems(6), sems(6), sems(15), sems(15), sems(6), sems(6), sems(8),
        sems(6), sems(6), sems(2), sems(30), pltpu.SemaphoreType.REGULAR((3,)),
    ]
    in_place = pl.BlockSpec(memory_space=pltpu.HBM)
    return pl.pallas_call(
        kernel,
        out_shape=jax.ShapeDtypeStruct(merged_vectors.shape, F32),
        in_specs=[in_place] * 4,
        out_specs=pl.BlockSpec(memory_space=pltpu.VMEM),
        scratch_shapes=scratch,
        compiler_params=pltpu.CompilerParams(
            collective_id=0, has_side_effects=True, vmem_limit_bytes=56 * 1024 * 1024
        ),
        name="back_transform",
    )(deflation, merged_vectors, vectors, factors)


def solution(mesh):
    in_specs = (P("col", "row"), P(), P(None, ("row", "col"), None), P())
    out_specs = P("col", "row")
    return jax.shard_map(
        per_device, mesh=mesh, in_specs=in_specs, out_specs=out_specs, check_vma=False
    )
```

```python
import jax
import jax.numpy as jnp
from jax import lax
from jax.experimental import pallas as pl
from jax.experimental.pallas import tpu as pltpu
from jax.sharding import PartitionSpec as P

MESH = pl.DeviceIdType.MESH
F32, BF16 = jnp.float32, jnp.bfloat16
YN, XN, ZN = 4, 4, 16
NB = 256
BLOCKS = 4
ROWS = 32
SHARD = 200
HALF = 128
PAIRS = 3
PLAIN = (((1,), (0,)), ((), ()))
RIGHT = (((1,), (1,)), ((), ()))
LEFT = (((0,), (0,)), ((), ()))


def split_parts(values):
    upper = values.astype(BF16)
    return upper, (values - upper.astype(F32)).astype(BF16)


def dot(a, b, numbers):
    return lax.dot_general(a, b, numbers, preferred_element_type=F32)


def split_dot(a, b, numbers):
    return dot(a[0], b[0], numbers) + dot(a[0], b[1], numbers) + dot(a[1], b[0], numbers)


def split_dot_few(a, b, numbers):
    rows = a[0].shape[0]
    both = dot(jnp.concatenate(a, axis=0), b[0], numbers)
    return both[:rows] + dot(a[0], b[1], numbers) + both[rows:]


def device(z, x, y, core):
    return (z * 2 + x // 2, y * 4 + (x % 2) * 2 + core)


def send(src, dst, sems, index, where):
    pltpu.make_async_remote_copy(
        src_ref=src,
        dst_ref=dst,
        send_sem=sems.at[0, index],
        recv_sem=sems.at[1, index],
        device_id=where,
        device_id_type=MESH,
    ).start()


def wait_bytes(like, sem):
    pltpu.make_async_copy(like, like, sem).wait()


def padded(values):
    rows = jnp.concatenate([values, jnp.zeros((NB - SHARD, values.shape[1]), F32)], axis=0)
    return rows.reshape(2, HALF, values.shape[1])


def kernel(
    order_hbm, a_hbm, v_hbm, f_hbm, out_ref,
    order_ref, place_ref, a_ref, v_ref, f_ref,
    v_other, v_up, v_low, f_up, f_low,
    a_send, a_recv,
    p_part, p_in1, p_mid, p_in2, p_tiles, p_in3, p_own,
    g_part, g_in1, g_mid, g_in2, g_tiles, g_in3, g_own,
    g_give, g_keep, g_take, g_all, w_all, o_part, o_sides, o_both0, o_both1, o_send, o_recv,
    in_sems, v_sems, a_sems, p1_sems, p2_sems, p3_sems, p4_sems,
    g1_sems, g2_sems, g3_sems, g4_sems, g5_sems, g6_sems, g7_sems,
    w1_sems, w2_sems, oc_sems, o_sems, known_sems,
):
    row = lax.axis_index("row")
    col = lax.axis_index("col")
    z, y, core = row // 2, col // 4, col % 2
    x_low = (col // 2) % 2
    x = (row % 2) * 2 + x_low
    chip = y * 2 + x_low
    sent = []

    def sending(like, sems, index):
        sent.append((like, sems.at[0, index]))
        return like, sems.at[1, index]

    def wait_sent():
        for like, sem in sent:
            wait_bytes(like, sem)
        sent.clear()

    y_peers = [(d, (y + d) % YN, device(z, x, (y + d) % YN, core)) for d in (2, 1, 3)]
    x_peers = [(d, (x + d) % XN, device(z, (x + d) % XN, y, core)) for d in (2, 1, 3)]
    far_first = sorted(range(1, ZN), key=lambda d: -min(d, ZN - d))
    z_peers = [(d, (z + d) % ZN, device((z + d) % ZN, x, y, core)) for d in far_first]
    group = []
    for dy in (2, 1, 3, 0):
        for dx in (1, 0):
            for dc in (1, 0):
                group.append(((y + dy) % YN, (x_low + dx) % 2, (core + dc) % 2))
    col_peers = [(row, gy * 4 + gx * 2 + gc) for gy, gx, gc in group[:-1]]
    far_x = [device(z, (x // 2 * 2 + 2) % XN + h, y, core) for h in range(2)]
    other_core = (row, y * 4 + x_low * 2 + 1 - core)

    barrier = pltpu.get_barrier_semaphore()
    near_z = [device((z + d) % ZN, x, y, core) for d in (1, ZN - 1)]
    peers = col_peers + far_x + near_z
    for peer in peers:
        pl.semaphore_signal(barrier, inc=1, device_id=peer, device_id_type=MESH)

    def tell(step):
        for d in (1 << step, ZN - (1 << step)):
            where = device((z + d) % ZN, x, y, core)
            pl.semaphore_signal(known_sems.at[step], inc=1, device_id=where, device_id_type=MESH)

    def hear(step):
        pl.semaphore_wait(known_sems.at[step], 2)

    inputs = [
        pltpu.make_async_copy(src, dst, in_sems.at[i])
        for i, (src, dst) in enumerate(
            ((v_hbm, v_ref), (a_hbm, a_ref), (f_hbm, f_ref), (order_hbm, order_ref))
        )
    ]
    for copy in inputs:
        copy.start()

    inputs[0].wait()
    for b in range(BLOCKS):
        up, low = split_parts(padded(v_ref[b]))
        v_up[b, :, core] = up
        v_low[b, :, core] = low

    def own_parts(b):
        return v_up[b, :, core].reshape(NB, NB), v_low[b, :, core].reshape(NB, NB)

    for to, into in ((1 - core, g_give), (core, g_keep)):
        lefts = (3, 3 - to, 2 - to)
        rights = (2 - 2 * to, 1 - to, 1 - to)
        for j in range(PAIRS):
            into[j] = split_dot(own_parts(lefts[j]), own_parts(rights[j]), LEFT)
    pl.semaphore_wait(barrier, len(peers))
    tell(0)
    send(g_give, g_take, v_sems, 1, other_core)
    g_copy = sending(g_take, v_sems, 1)
    send(v_ref, v_other, v_sems, 0, other_core)
    v_copy = sending(v_other, v_sems, 0)
    inputs[1].wait()
    a_value = a_ref[...]
    gap = jnp.zeros((ROWS, NB - SHARD), F32)
    for s in range(8):
        first, second = s * 2 * SHARD, (s * 2 + 1) * SHARD
        pieces = [
            a_value[:, first : first + HALF],
            a_value[:, second : second + HALF],
            a_value[:, first + HALF : first + SHARD],
            gap,
            a_value[:, second + HALF : second + SHARD],
            gap,
        ]
        a_send[s] = jnp.concatenate(pieces, axis=1)
    a_recv[chip] = a_send[chip]
    for gy, gx, _ in group[1:-1:2]:
        where = (row, gy * 4 + gx * 2 + core)
        send(a_send.at[gy * 2 + gx], a_recv.at[chip], a_sems, 0, where)
    a_copies = sending(a_recv.at[pl.ds(0, 7)], a_sems, 0)

    def v_parts(b):
        return v_up[b].reshape(2 * NB, NB), v_low[b].reshape(2 * NB, NB)

    def start_first(half, part, into, sems):
        for d, place, peer in (y_peers, x_peers)[half]:
            src = part.at[0, :, place] if half == 0 else part.at[1, :, :, place]
            send(src, into.at[half, d - 1], sems, half, peer)
        return sending(into.at[half], sems, half)

    def finish_first(half, copies, part, into, mid):
        wait_bytes(*copies)
        own = part[0, :, y] if half == 0 else part[1, :, :, x]
        mid[half] = own + into[half, 0] + into[half, 1] + into[half, 2]

    def start_second(half, mid, into, sems):
        for d, place, peer in (x_peers, y_peers)[half]:
            send(mid.at[half, :, place], into.at[half, d - 1], sems, half, peer)
        return sending(into.at[half], sems, half)

    def finish_second(half, copies, mid, into, tiles):
        wait_bytes(*copies)
        value = mid[half, :, (x, y)[half]] + into[half, 0] + into[half, 1] + into[half, 2]
        count, lanes = value.shape[0], value.shape[2] // 128
        for t in range(count * 2 * lanes):
            j, g, h = t // (2 * lanes), t // lanes % 2, t % lanes
            piece = value[j, g * 8 : g * 8 + 8, h * 128 : h * 128 + 128]
            tiles[half * count * 2 * lanes + t] = piece

    def start_z(tiles, into, sems):
        for d, place, peer in z_peers:
            send(tiles.at[place], into.at[d - 1], sems, 0, peer)
        return sending(into, sems, 0)

    def finish_z(copies, tiles, into, own):
        wait_bytes(*copies)
        own[z] = tiles[z] + jnp.sum(into[...], axis=0)

    def start_z_back(own, sems):
        for _, _, peer in z_peers:
            send(own.at[z], own.at[z], sems, 0, peer)
        return sending(own.at[pl.ds(0, ZN - 1)], sems, 0)

    def finish_z_back(copies, own, count, lanes):
        wait_bytes(*copies)
        blocks = []
        for j in range(2 * count):
            base = j * 2 * lanes
            halves = [
                jnp.concatenate([own[base + g * lanes + h] for h in range(lanes)], axis=1)
                for g in range(2)
            ]
            blocks.append(jnp.concatenate(halves, axis=0))
        return blocks

    def start_back(half, whole, sems):
        mine = whole.at[half, :, y, x]
        for _, _, peer in (x_peers, y_peers)[half]:
            send(mine, mine, sems, half, peer)
        return sending(whole.at[half, :, 0, pl.ds(0, 3)], sems, half)

    def finish_back(half, whole, copies, sems):
        wait_bytes(*copies)
        mine = whole.at[0, :, y] if half == 0 else whole.at[1, :, :, x]
        for _, _, peer in (y_peers, x_peers)[half]:
            send(mine, mine, sems, half, peer)
        return sending(whole.at[half, :, pl.ds(0, 3)], sems, half)

    wait_bytes(*g_copy)
    for j in range(PAIRS):
        product = g_keep[j] + g_take[j]
        for half in range(2):
            lanes = product[:, half * 128 : half * 128 + 128]
            g_part[half, j] = lanes.reshape(YN, XN, 16, 128)
    g1 = [start_first(half, g_part, g_in1, g1_sems) for half in range(2)]
    hear(0)
    tell(1)
    wait_bytes(*v_copy)
    for b in range(BLOCKS):
        up, low = split_parts(padded(v_other[b]))
        v_up[b, :, 1 - core] = up
        v_low[b, :, 1 - core] = low
    hear(1)
    tell(2)

    g2 = []
    for half in range(2):
        finish_first(half, g1[half], g_part, g_in1, g_mid)
        g2.append(start_second(half, g_mid, g_in2, g2_sems))

    wait_bytes(*a_copies)
    a_parts = split_parts(a_recv[...].reshape(8 * ROWS, 2 * NB))
    p1 = []
    for half in range(2):
        for i in range(2):
            product = split_dot(a_parts, v_parts(3 - 2 * half - i), PLAIN)
            p_part[half, i] = product.reshape(YN, XN, 16, NB)
        p1.append(start_first(half, p_part, p_in1, p1_sems))

    for half in range(2):
        finish_second(half, g2[half], g_mid, g_in2, g_tiles)
    for t in range(12, ZN):
        g_tiles[t] = jnp.zeros((8, 128), F32)
    hear(2)
    g3 = start_z(g_tiles, g_in3, g3_sems)

    inputs[2].wait()
    for b in range(BLOCKS):
        up, low = split_parts(f_ref[b])
        f_up[b] = up
        f_low[b] = low
    inputs[3].wait()

    @pl.loop(0, 16 * ROWS, unroll=8)
    def _(k):
        source = order_ref[k]
        place_ref[k] = (source >> 5 & 1) * (8 * ROWS) + (source >> 6) * ROWS + (source & 31)

    p2 = []
    for half in range(2):
        finish_first(half, p1[half], p_part, p_in1, p_mid)
        p2.append(start_second(half, p_mid, p_in2, p2_sems))
    finish_z(g3, g_tiles, g_in3, g_own)
    g4 = start_z_back(g_own, g4_sems)
    for half in range(2):
        finish_second(half, p2[half], p_mid, p_in2, p_tiles)
    p3 = start_z(p_tiles, p_in3, p3_sems)

    g_mine = g_all.at[core]
    for j, block in enumerate(finish_z_back(g4, g_own, PAIRS, 1)):
        g_all[core, j // PAIRS, j % PAIRS, y, x] = block
    g5 = [start_back(half, g_mine, g5_sems) for half in range(2)]
    finish_z(p3, p_tiles, p_in3, p_own)
    p4 = start_z_back(p_own, p4_sems)
    g6 = [finish_back(half, g_mine, g5[half], g6_sems) for half in range(2)]
    g7 = []
    for half in range(2):
        wait_bytes(*g6[half])
        send(g_mine.at[half], g_mine.at[half], g7_sems, half, other_core)
        g7.append(sending(g_mine.at[half], g7_sems, half))

    proj = finish_z_back(p4, p_own, 2, 2)
    w = [None] * BLOCKS
    w[0] = split_dot(split_parts(proj[0]), (f_up[3], f_low[3]), RIGHT)
    for copy in g7:
        wait_bytes(*copy)

    def g_parts(c, j):
        block = jnp.concatenate(
            [g_all[c, half, j].reshape(NB, 128) for half in range(2)], axis=1
        )
        return split_parts(block)

    places = {(0, 1): (0, 0), (0, 2): (0, 1), (1, 2): (0, 2), (0, 3): (1, 0), (1, 3): (1, 1), (2, 3): (1, 2)}
    w_parts = [split_parts(w[0])]
    w_all[0, 0, y, x] = w[0]
    w1 = []
    for i in range(1, BLOCKS):
        value = proj[i]
        for k in range(i):
            value = value - split_dot(w_parts[k], g_parts(*places[k, i]), PLAIN)
        value = split_dot(split_parts(value), (f_up[3 - i], f_low[3 - i]), RIGHT)
        w_parts.append(split_parts(value))
        w_all[i // 2, i % 2, y, x] = value
        if i % 2 == 1:
            w1.append(start_back(i // 2, w_all, w1_sems))
    w2 = [finish_back(half, w_all, w1[half], w2_sems) for half in range(2)]

    w_blocks = {}
    o_both = (o_both0, o_both1)
    for part in range(2):
        o_part[part] = a_recv[:, :, part * NB : part * NB + NB].reshape(8 * ROWS, NB)
    oc = []
    for half in range(2):
        wait_bytes(*w2[half])
        for i in range(2):
            w_blocks[half, i] = split_parts(w_all[half, i].reshape(8 * ROWS, NB))
        for part in range(2):
            value = o_part[part]
            for i in range(2):
                b = 3 - 2 * half - i
                v_block = (v_up[b, part].reshape(NB, NB), v_low[b, part].reshape(NB, NB))
                value = value - split_dot(w_blocks[half, i], v_block, RIGHT)
            if half == 0:
                o_part[part] = value
            else:
                for side in range(2):
                    o_sides[part, side] = value[:, side * HALF : side * HALF + HALF]
                into = o_both[part].at[pl.ds(core * 8 * ROWS, 8 * ROWS)]
                send(o_sides.at[part, 1 - core], into, oc_sems, part, other_core)
                oc.append(sending(o_sides.at[part, 1 - core], oc_sems, part))
                o_both[part][pl.ds(core * 8 * ROWS, 8 * ROWS)] = o_sides[part, core]
    o_copies = []
    for part in range(2):
        wait_bytes(*oc[part])
        for i, (ty, tx, tc) in enumerate(group):
            target = ty * 4 + tx * 2 + tc

            @pl.loop(0, ROWS, unroll=16)
            def _(k):
                place = place_ref[target * ROWS + k]
                o_send[part, target, pl.ds(k, 1), :] = o_both[part][pl.ds(place, 1), :]

            if i < 15:
                src, dst = o_send.at[part, target], o_recv.at[part, col]
                send(src, dst, o_sems, part, (row, target))
        o_copies.append(sending(o_recv.at[part, pl.ds(0, 15)], o_sems, part))
    for part in range(2):
        o_recv[part, col] = o_send[part, col]
    wait_sent()
    for copy in o_copies:
        wait_bytes(*copy)
    for c in range(16):
        out_ref[:, c * SHARD : c * SHARD + HALF] = o_recv[0, c]
        out_ref[:, c * SHARD + HALF : c * SHARD + SHARD] = o_recv[1, c][:, : SHARD - HALF]


def vmem(*shape):
    return pltpu.VMEM(shape, F32)


def half_vmem(*shape):
    return pltpu.VMEM(shape, BF16)


def sems(count):
    return pltpu.SemaphoreType.DMA((2, count))


def reduce_bufs(n, lanes):
    return [
        vmem(2, n, YN, XN, 16, lanes), vmem(2, 3, n, 4, 16, lanes), vmem(2, n, 4, 16, lanes),
        vmem(2, 3, n, 16, lanes), vmem(ZN, 8, 128), vmem(ZN - 1, 8, 128), vmem(ZN, 8, 128),
    ]


def per_device(merged_vectors, deflation, vectors, factors):
    rows = 8 * ROWS
    scratch = [
        pltpu.SMEM(deflation.shape, jnp.int32), pltpu.SMEM(deflation.shape, jnp.int32),
        vmem(*merged_vectors.shape),
        vmem(*vectors.shape), vmem(*factors.shape),
        vmem(BLOCKS, SHARD, NB),
        half_vmem(BLOCKS, 2, 2, HALF, NB), half_vmem(BLOCKS, 2, 2, HALF, NB),
        half_vmem(BLOCKS, NB, NB), half_vmem(BLOCKS, NB, NB),
        vmem(8, ROWS, 2 * NB), vmem(8, ROWS, 2 * NB),
        *reduce_bufs(2, NB),
        *reduce_bufs(PAIRS, 128),
        vmem(PAIRS, NB, NB), vmem(PAIRS, NB, NB), vmem(PAIRS, NB, NB),
        vmem(2, 2, PAIRS, YN, XN, 16, 128),
        vmem(2, 2, YN, XN, 16, NB),
        vmem(2, rows, NB), vmem(2, 2, rows, HALF), vmem(2 * rows, HALF), vmem(2 * rows, HALF),
        vmem(2, 16, ROWS, HALF), vmem(2, 16, ROWS, HALF),
        pltpu.SemaphoreType.DMA((4,)),
        sems(2), sems(1), sems(2), sems(2), sems(1), sems(1),
        sems(2), sems(2), sems(1), sems(1), sems(2), sems(2), sems(2),
        sems(2), sems(2), sems(2), sems(2), pltpu.SemaphoreType.REGULAR((3,)),
    ]
    in_place = pl.BlockSpec(memory_space=pltpu.HBM)
    return pl.pallas_call(
        kernel,
        out_shape=jax.ShapeDtypeStruct(merged_vectors.shape, F32),
        in_specs=[in_place] * 4,
        out_specs=pl.BlockSpec(memory_space=pltpu.VMEM),
        scratch_shapes=scratch,
        compiler_params=pltpu.CompilerParams(
            collective_id=0, has_side_effects=True, vmem_limit_bytes=56 * 1024 * 1024
        ),
        name="back_transform",
    )(deflation, merged_vectors, vectors, factors)


def solution(mesh):
    in_specs = (P("col", "row"), P(), P(None, ("row", "col"), None), P())
    out_specs = P("col", "row")
    return jax.shard_map(
        per_device, mesh=mesh, in_specs=in_specs, out_specs=out_specs, check_vma=False
    )
```

```python
import jax
import jax.numpy as jnp
from jax import lax
from jax.experimental import pallas as pl
from jax.experimental.pallas import tpu as pltpu
from jax.sharding import PartitionSpec as P

MESH = pl.DeviceIdType.MESH
F32, BF16 = jnp.float32, jnp.bfloat16
YN, XN, ZN = 4, 4, 16
NB = 256
BLOCKS = 4
ROWS = 32
SHARD = 200
HALF = 128
PAIRS = 3
PLAIN = (((1,), (0,)), ((), ()))
RIGHT = (((1,), (1,)), ((), ()))
LEFT = (((0,), (0,)), ((), ()))


def split_parts(values):
    upper = values.astype(BF16)
    return upper, (values - upper.astype(F32)).astype(BF16)


def dot(a, b, numbers):
    return lax.dot_general(a, b, numbers, preferred_element_type=F32)


def split_dot(a, b, numbers):
    return dot(a[0], b[0], numbers) + dot(a[0], b[1], numbers) + dot(a[1], b[0], numbers)


def device(z, x, y, core):
    return (z * 2 + x // 2, y * 4 + (x % 2) * 2 + core)


def send(src, dst, sems, index, where):
    pltpu.make_async_remote_copy(
        src_ref=src,
        dst_ref=dst,
        send_sem=sems.at[0, index],
        recv_sem=sems.at[1, index],
        device_id=where,
        device_id_type=MESH,
    ).start()


def wait_bytes(like, sem):
    pltpu.make_async_copy(like, like, sem).wait()


def padded(values):
    rows = jnp.concatenate([values, jnp.zeros((NB - SHARD, values.shape[1]), F32)], axis=0)
    return rows.reshape(2, HALF, values.shape[1])


def kernel(
    order_hbm, a_hbm, v_hbm, f_hbm, out_ref,
    order_ref, place_ref, a_ref, v_ref, f_ref,
    v_other, v_up, v_low, f_up, f_low,
    a_send, a_recv,
    p_part, p_in1, p_mid, p_in2, p_tiles, p_in3, p_own,
    g_part, g_in1, g_mid, g_in2, g_tiles, g_in3, g_own,
    g_give, g_keep, g_take, g_all, p_all, o_part, o_sides, o_both0, o_both1, o_send, o_recv,
    in_sems, v_sems, a_sems, p1_sems, p2_sems, p3_sems, p4_sems,
    g1_sems, g2_sems, g3_sems, g4_sems, g5_sems, g6_sems, g7_sems,
    p5_sems, p6_sems, oc_sems, o_sems, known_sems,
):
    row = lax.axis_index("row")
    col = lax.axis_index("col")
    z, y, core = row // 2, col // 4, col % 2
    x_low = (col // 2) % 2
    x = (row % 2) * 2 + x_low
    chip = y * 2 + x_low
    sent = []

    def sending(like, sems, index):
        sent.append((like, sems.at[0, index]))
        return like, sems.at[1, index]

    def wait_sent():
        for like, sem in sent:
            wait_bytes(like, sem)
        sent.clear()

    y_peers = [(d, (y + d) % YN, device(z, x, (y + d) % YN, core)) for d in (2, 1, 3)]
    x_peers = [(d, (x + d) % XN, device(z, (x + d) % XN, y, core)) for d in (2, 1, 3)]
    far_first = sorted(range(1, ZN), key=lambda d: -min(d, ZN - d))
    z_peers = [(d, (z + d) % ZN, device((z + d) % ZN, x, y, core)) for d in far_first]
    group = []
    for dy in (2, 1, 3, 0):
        for dx in (1, 0):
            for dc in (1, 0):
                group.append(((y + dy) % YN, (x_low + dx) % 2, (core + dc) % 2))
    col_peers = [(row, gy * 4 + gx * 2 + gc) for gy, gx, gc in group[:-1]]
    far_x = [device(z, (x // 2 * 2 + 2) % XN + h, y, core) for h in range(2)]
    other_core = (row, y * 4 + x_low * 2 + 1 - core)

    barrier = pltpu.get_barrier_semaphore()
    near_z = [device((z + d) % ZN, x, y, core) for d in (1, ZN - 1)]
    peers = col_peers + far_x + near_z
    for peer in peers:
        pl.semaphore_signal(barrier, inc=1, device_id=peer, device_id_type=MESH)

    def tell(step):
        for d in (1 << step, ZN - (1 << step)):
            where = device((z + d) % ZN, x, y, core)
            pl.semaphore_signal(known_sems.at[step], inc=1, device_id=where, device_id_type=MESH)

    def hear(step):
        pl.semaphore_wait(known_sems.at[step], 2)

    inputs = [
        pltpu.make_async_copy(src, dst, in_sems.at[i])
        for i, (src, dst) in enumerate(
            ((v_hbm, v_ref), (a_hbm, a_ref), (f_hbm, f_ref), (order_hbm, order_ref))
        )
    ]
    for copy in inputs:
        copy.start()

    inputs[0].wait()
    for b in range(BLOCKS):
        up, low = split_parts(padded(v_ref[b]))
        v_up[b, :, core] = up
        v_low[b, :, core] = low

    def own_parts(b):
        return v_up[b, :, core].reshape(NB, NB), v_low[b, :, core].reshape(NB, NB)

    for to, into in ((1 - core, g_give), (core, g_keep)):
        lefts = (3, 3 - to, 2 - to)
        rights = (2 - 2 * to, 1 - to, 1 - to)
        for j in range(PAIRS):
            into[j] = split_dot(own_parts(lefts[j]), own_parts(rights[j]), LEFT)
    pl.semaphore_wait(barrier, len(peers))
    tell(0)
    send(g_give, g_take, v_sems, 1, other_core)
    g_copy = sending(g_take, v_sems, 1)
    send(v_ref, v_other, v_sems, 0, other_core)
    v_copy = sending(v_other, v_sems, 0)
    inputs[1].wait()
    a_value = a_ref[...]
    gap = jnp.zeros((ROWS, NB - SHARD), F32)
    for s in range(8):
        first, second = s * 2 * SHARD, (s * 2 + 1) * SHARD
        pieces = [
            a_value[:, first : first + HALF],
            a_value[:, second : second + HALF],
            a_value[:, first + HALF : first + SHARD],
            gap,
            a_value[:, second + HALF : second + SHARD],
            gap,
        ]
        a_send[s] = jnp.concatenate(pieces, axis=1)
    a_recv[chip] = a_send[chip]
    for gy, gx, _ in group[1:-1:2]:
        where = (row, gy * 4 + gx * 2 + core)
        send(a_send.at[gy * 2 + gx], a_recv.at[chip], a_sems, 0, where)
    a_copies = sending(a_recv.at[pl.ds(0, 7)], a_sems, 0)

    def v_parts(b):
        return v_up[b].reshape(2 * NB, NB), v_low[b].reshape(2 * NB, NB)

    def start_first(half, part, into, sems):
        for d, place, peer in (y_peers, x_peers)[half]:
            src = part.at[0, :, place] if half == 0 else part.at[1, :, :, place]
            send(src, into.at[half, d - 1], sems, half, peer)
        return sending(into.at[half], sems, half)

    def finish_first(half, copies, part, into, mid):
        wait_bytes(*copies)
        own = part[0, :, y] if half == 0 else part[1, :, :, x]
        mid[half] = own + into[half, 0] + into[half, 1] + into[half, 2]

    def start_second(half, mid, into, sems):
        for d, place, peer in (x_peers, y_peers)[half]:
            send(mid.at[half, :, place], into.at[half, d - 1], sems, half, peer)
        return sending(into.at[half], sems, half)

    def finish_second(half, copies, mid, into, tiles):
        wait_bytes(*copies)
        value = mid[half, :, (x, y)[half]] + into[half, 0] + into[half, 1] + into[half, 2]
        count, lanes = value.shape[0], value.shape[2] // 128
        for t in range(count * 2 * lanes):
            j, g, h = t // (2 * lanes), t // lanes % 2, t % lanes
            piece = value[j, g * 8 : g * 8 + 8, h * 128 : h * 128 + 128]
            tiles[half * count * 2 * lanes + t] = piece

    def start_z(tiles, into, sems):
        for d, place, peer in z_peers:
            send(tiles.at[place], into.at[d - 1], sems, 0, peer)
        return sending(into, sems, 0)

    def finish_z(copies, tiles, into, own):
        wait_bytes(*copies)
        own[z] = tiles[z] + jnp.sum(into[...], axis=0)

    def start_z_back(own, sems):
        for _, _, peer in z_peers:
            send(own.at[z], own.at[z], sems, 0, peer)
        return sending(own.at[pl.ds(0, ZN - 1)], sems, 0)

    def finish_z_back(copies, own, count, lanes):
        wait_bytes(*copies)
        blocks = []
        for j in range(2 * count):
            base = j * 2 * lanes
            halves = [
                jnp.concatenate([own[base + g * lanes + h] for h in range(lanes)], axis=1)
                for g in range(2)
            ]
            blocks.append(jnp.concatenate(halves, axis=0))
        return blocks

    def start_back(half, whole, sems):
        mine = whole.at[half, :, y, x]
        for _, _, peer in (x_peers, y_peers)[half]:
            send(mine, mine, sems, half, peer)
        return sending(whole.at[half, :, 0, pl.ds(0, 3)], sems, half)

    def finish_back(half, whole, copies, sems):
        wait_bytes(*copies)
        mine = whole.at[0, :, y] if half == 0 else whole.at[1, :, :, x]
        for _, _, peer in (y_peers, x_peers)[half]:
            send(mine, mine, sems, half, peer)
        return sending(whole.at[half, :, pl.ds(0, 3)], sems, half)

    wait_bytes(*g_copy)
    for j in range(PAIRS):
        product = g_keep[j] + g_take[j]
        for half in range(2):
            lanes = product[:, half * 128 : half * 128 + 128]
            g_part[half, j] = lanes.reshape(YN, XN, 16, 128)
    g1 = [start_first(half, g_part, g_in1, g1_sems) for half in range(2)]
    hear(0)
    tell(1)
    wait_bytes(*v_copy)
    for b in range(BLOCKS):
        up, low = split_parts(padded(v_other[b]))
        v_up[b, :, 1 - core] = up
        v_low[b, :, 1 - core] = low
    hear(1)
    tell(2)

    g2 = []
    for half in range(2):
        finish_first(half, g1[half], g_part, g_in1, g_mid)
        g2.append(start_second(half, g_mid, g_in2, g2_sems))

    wait_bytes(*a_copies)
    a_parts = split_parts(a_recv[...].reshape(8 * ROWS, 2 * NB))
    p1 = []
    for half in range(2):
        for i in range(2):
            product = split_dot(a_parts, v_parts(3 - 2 * half - i), PLAIN)
            p_part[half, i] = product.reshape(YN, XN, 16, NB)
        p1.append(start_first(half, p_part, p_in1, p1_sems))

    for half in range(2):
        finish_second(half, g2[half], g_mid, g_in2, g_tiles)
    for t in range(12, ZN):
        g_tiles[t] = jnp.zeros((8, 128), F32)
    hear(2)
    g3 = start_z(g_tiles, g_in3, g3_sems)

    inputs[2].wait()
    for b in range(BLOCKS):
        up, low = split_parts(f_ref[b])
        f_up[b] = up
        f_low[b] = low
    inputs[3].wait()

    @pl.loop(0, 16 * ROWS, unroll=8)
    def _(k):
        source = order_ref[k]
        place_ref[k] = (source >> 5 & 1) * (8 * ROWS) + (source >> 6) * ROWS + (source & 31)

    p2 = []
    for half in range(2):
        finish_first(half, p1[half], p_part, p_in1, p_mid)
        p2.append(start_second(half, p_mid, p_in2, p2_sems))
    finish_z(g3, g_tiles, g_in3, g_own)
    g4 = start_z_back(g_own, g4_sems)
    for half in range(2):
        finish_second(half, p2[half], p_mid, p_in2, p_tiles)
    p3 = start_z(p_tiles, p_in3, p3_sems)

    g_mine = g_all.at[core]
    for j, block in enumerate(finish_z_back(g4, g_own, PAIRS, 1)):
        g_all[core, j // PAIRS, j % PAIRS, y, x] = block
    g5 = [start_back(half, g_mine, g5_sems) for half in range(2)]
    finish_z(p3, p_tiles, p_in3, p_own)
    p4 = start_z_back(p_own, p4_sems)
    g6 = [finish_back(half, g_mine, g5[half], g6_sems) for half in range(2)]

    for i, block in enumerate(finish_z_back(p4, p_own, 2, 2)):
        p_all[i // 2, i % 2, y, x] = block
    p5 = [start_back(half, p_all, p5_sems) for half in range(2)]
    g7 = []
    for half in range(2):
        wait_bytes(*g6[half])
        send(g_mine.at[half], g_mine.at[half], g7_sems, half, other_core)
        g7.append(sending(g_mine.at[half], g7_sems, half))
    p6 = [finish_back(half, p_all, p5[half], p6_sems) for half in range(2)]

    for part in range(2):
        o_part[part] = a_recv[:, :, part * NB : part * NB + NB].reshape(8 * ROWS, NB)

    def projected(i):
        return p_all[i // 2, i % 2].reshape(8 * ROWS, NB)

    def combine(value, i):
        return split_parts(split_dot(split_parts(value), (f_up[3 - i], f_low[3 - i]), RIGHT))

    def subtract(i, part):
        v_block = (v_up[3 - i, part].reshape(NB, NB), v_low[3 - i, part].reshape(NB, NB))
        return o_part[part] - split_dot(w_parts[i], v_block, RIGHT)

    wait_bytes(*p6[0])
    w_parts = [combine(projected(0), 0)]
    for part in range(2):
        o_part[part] = subtract(0, part)
    for copy in g7:
        wait_bytes(*copy)
    wait_bytes(*p6[1])

    def g_parts(c, j):
        block = jnp.concatenate(
            [g_all[c, half, j].reshape(NB, 128) for half in range(2)], axis=1
        )
        return split_parts(block)

    places = {(0, 1): (0, 0), (0, 2): (0, 1), (1, 2): (0, 2), (0, 3): (1, 0), (1, 3): (1, 1), (2, 3): (1, 2)}
    for i in range(1, BLOCKS):
        value = projected(i)
        for k in range(i):
            value = value - split_dot(w_parts[k], g_parts(*places[k, i]), PLAIN)
        w_parts.append(combine(value, i))
        if i < BLOCKS - 1:
            for part in range(2):
                o_part[part] = subtract(i, part)

    o_both = (o_both0, o_both1)
    oc = []
    for part in range(2):
        value = subtract(BLOCKS - 1, part)
        for side in range(2):
            o_sides[part, side] = value[:, side * HALF : side * HALF + HALF]
        into = o_both[part].at[pl.ds(core * 8 * ROWS, 8 * ROWS)]
        send(o_sides.at[part, 1 - core], into, oc_sems, part, other_core)
        oc.append(sending(o_sides.at[part, 1 - core], oc_sems, part))
        o_both[part][pl.ds(core * 8 * ROWS, 8 * ROWS)] = o_sides[part, core]
    o_copies = []
    for part in range(2):
        wait_bytes(*oc[part])
        for i, (ty, tx, tc) in enumerate(group):
            target = ty * 4 + tx * 2 + tc

            @pl.loop(0, ROWS, unroll=16)
            def _(k):
                place = place_ref[target * ROWS + k]
                o_send[part, target, pl.ds(k, 1), :] = o_both[part][pl.ds(place, 1), :]

            if i < 15:
                src, dst = o_send.at[part, target], o_recv.at[part, col]
                send(src, dst, o_sems, part, (row, target))
        o_copies.append(sending(o_recv.at[part, pl.ds(0, 15)], o_sems, part))
    for part in range(2):
        o_recv[part, col] = o_send[part, col]
    wait_sent()
    for copy in o_copies:
        wait_bytes(*copy)
    for c in range(16):
        out_ref[:, c * SHARD : c * SHARD + HALF] = o_recv[0, c]
        out_ref[:, c * SHARD + HALF : c * SHARD + SHARD] = o_recv[1, c][:, : SHARD - HALF]


def vmem(*shape):
    return pltpu.VMEM(shape, F32)


def half_vmem(*shape):
    return pltpu.VMEM(shape, BF16)


def sems(count):
    return pltpu.SemaphoreType.DMA((2, count))


def reduce_bufs(n, lanes):
    return [
        vmem(2, n, YN, XN, 16, lanes), vmem(2, 3, n, 4, 16, lanes), vmem(2, n, 4, 16, lanes),
        vmem(2, 3, n, 16, lanes), vmem(ZN, 8, 128), vmem(ZN - 1, 8, 128), vmem(ZN, 8, 128),
    ]


def per_device(merged_vectors, deflation, vectors, factors):
    rows = 8 * ROWS
    scratch = [
        pltpu.SMEM(deflation.shape, jnp.int32), pltpu.SMEM(deflation.shape, jnp.int32),
        vmem(*merged_vectors.shape),
        vmem(*vectors.shape), vmem(*factors.shape),
        vmem(BLOCKS, SHARD, NB),
        half_vmem(BLOCKS, 2, 2, HALF, NB), half_vmem(BLOCKS, 2, 2, HALF, NB),
        half_vmem(BLOCKS, NB, NB), half_vmem(BLOCKS, NB, NB),
        vmem(8, ROWS, 2 * NB), vmem(8, ROWS, 2 * NB),
        *reduce_bufs(2, NB),
        *reduce_bufs(PAIRS, 128),
        vmem(PAIRS, NB, NB), vmem(PAIRS, NB, NB), vmem(PAIRS, NB, NB),
        vmem(2, 2, PAIRS, YN, XN, 16, 128),
        vmem(2, 2, YN, XN, 16, NB),
        vmem(2, rows, NB), vmem(2, 2, rows, HALF), vmem(2 * rows, HALF), vmem(2 * rows, HALF),
        vmem(2, 16, ROWS, HALF), vmem(2, 16, ROWS, HALF),
        pltpu.SemaphoreType.DMA((4,)),
        sems(2), sems(1), sems(2), sems(2), sems(1), sems(1),
        sems(2), sems(2), sems(1), sems(1), sems(2), sems(2), sems(2),
        sems(2), sems(2), sems(2), sems(2), pltpu.SemaphoreType.REGULAR((3,)),
    ]
    in_place = pl.BlockSpec(memory_space=pltpu.HBM)
    return pl.pallas_call(
        kernel,
        out_shape=jax.ShapeDtypeStruct(merged_vectors.shape, F32),
        in_specs=[in_place] * 4,
        out_specs=pl.BlockSpec(memory_space=pltpu.VMEM),
        scratch_shapes=scratch,
        compiler_params=pltpu.CompilerParams(
            collective_id=0, has_side_effects=True, vmem_limit_bytes=56 * 1024 * 1024
        ),
        name="back_transform",
    )(deflation, merged_vectors, vectors, factors)


def solution(mesh):
    in_specs = (P("col", "row"), P(), P(None, ("row", "col"), None), P())
    out_specs = P("col", "row")
    return jax.shard_map(
        per_device, mesh=mesh, in_specs=in_specs, out_specs=out_specs, check_vma=False
    )
```

```python
import jax
import jax.numpy as jnp
from jax import lax
from jax.experimental import pallas as pl
from jax.experimental.pallas import tpu as pltpu
from jax.sharding import PartitionSpec as P

MESH = pl.DeviceIdType.MESH
F32, BF16 = jnp.float32, jnp.bfloat16
YN, XN, ZN = 4, 4, 16
NB = 256
BLOCKS = 4
ROWS = 32
SHARD = 200
HALF = 128
PAIRS = 3
PLAIN = (((1,), (0,)), ((), ()))
RIGHT = (((1,), (1,)), ((), ()))
LEFT = (((0,), (0,)), ((), ()))


def split_parts(values):
    upper = values.astype(BF16)
    return upper, (values - upper.astype(F32)).astype(BF16)


def dot(a, b, numbers):
    return lax.dot_general(a, b, numbers, preferred_element_type=F32)


def split_dot(a, b, numbers):
    return dot(a[0], b[0], numbers) + dot(a[0], b[1], numbers) + dot(a[1], b[0], numbers)


def device(z, x, y, core):
    return (z * 2 + x // 2, y * 4 + (x % 2) * 2 + core)


def send(src, dst, sems, index, where):
    pltpu.make_async_remote_copy(
        src_ref=src,
        dst_ref=dst,
        send_sem=sems.at[0, index],
        recv_sem=sems.at[1, index],
        device_id=where,
        device_id_type=MESH,
    ).start()


def wait_bytes(like, sem):
    pltpu.make_async_copy(like, like, sem).wait()


def padded(values):
    rows = jnp.concatenate([values, jnp.zeros((NB - SHARD, values.shape[1]), F32)], axis=0)
    return rows.reshape(2, HALF, values.shape[1])


def kernel(
    order_hbm, a_hbm, v_hbm, f_hbm, out_ref,
    order_ref, place_ref, a_ref, v_ref, f_ref,
    v_other, v_up, v_low, f_up, f_low,
    a_send, a_recv,
    p_part, p_in1, p_mid, p_in2, p_tiles, p_in3, p_own,
    g_part, g_in1, g_mid, g_in2, g_tiles, g_in3, g_own,
    g_give, g_keep, g_take, g_all, p_all, o_part, o_sides, o_both0, o_both1, o_send, o_recv,
    in_sems, v_sems, a_sems, p1_sems, p2_sems, p3_sems, p4_sems,
    g1_sems, g2_sems, g3_sems, g4_sems, g5_sems, g6_sems, g7_sems,
    p5_sems, p6_sems, oc_sems, o_sems, known_sems,
):
    row = lax.axis_index("row")
    col = lax.axis_index("col")
    z, y, core = row // 2, col // 4, col % 2
    x_low = (col // 2) % 2
    x = (row % 2) * 2 + x_low
    chip = y * 2 + x_low
    sent = []

    def sending(like, sems, index):
        sent.append((like, sems.at[0, index]))
        return like, sems.at[1, index]

    def wait_sent():
        for like, sem in sent:
            wait_bytes(like, sem)
        sent.clear()

    y_peers = [(d, (y + d) % YN, device(z, x, (y + d) % YN, core)) for d in (2, 1, 3)]
    x_peers = [(d, (x + d) % XN, device(z, (x + d) % XN, y, core)) for d in (2, 1, 3)]
    far_first = sorted(range(1, ZN), key=lambda d: -min(d, ZN - d))
    z_peers = [(d, (z + d) % ZN, device((z + d) % ZN, x, y, core)) for d in far_first]
    group = []
    for dy in (2, 1, 3, 0):
        for dx in (1, 0):
            for dc in (1, 0):
                group.append(((y + dy) % YN, (x_low + dx) % 2, (core + dc) % 2))
    col_peers = [(row, gy * 4 + gx * 2 + gc) for gy, gx, gc in group[:-1]]
    far_x = [device(z, (x // 2 * 2 + 2) % XN + h, y, core) for h in range(2)]
    other_core = (row, y * 4 + x_low * 2 + 1 - core)

    barrier = pltpu.get_barrier_semaphore()
    near_z = [device((z + d) % ZN, x, y, core) for d in (1, ZN - 1)]
    peers = col_peers + far_x + near_z
    for peer in peers:
        pl.semaphore_signal(barrier, inc=1, device_id=peer, device_id_type=MESH)

    def tell(step):
        for d in (1 << step, ZN - (1 << step)):
            where = device((z + d) % ZN, x, y, core)
            pl.semaphore_signal(known_sems.at[step], inc=1, device_id=where, device_id_type=MESH)

    def hear(step):
        pl.semaphore_wait(known_sems.at[step], 2)

    inputs = [
        pltpu.make_async_copy(src, dst, in_sems.at[i])
        for i, (src, dst) in enumerate(
            ((v_hbm, v_ref), (a_hbm, a_ref), (f_hbm, f_ref), (order_hbm, order_ref))
        )
    ]
    for copy in inputs:
        copy.start()

    inputs[0].wait()
    for b in range(BLOCKS):
        up, low = split_parts(padded(v_ref[b]))
        v_up[b, :, core] = up
        v_low[b, :, core] = low

    def own_parts(b):
        return v_up[b, :, core].reshape(NB, NB), v_low[b, :, core].reshape(NB, NB)

    for to, into in ((1 - core, g_give), (core, g_keep)):
        lefts = (3, 3 - to, 2 - to)
        rights = (2 - 2 * to, 1 - to, 1 - to)
        for j in range(PAIRS):
            into[j] = split_dot(own_parts(lefts[j]), own_parts(rights[j]), LEFT)
    pl.semaphore_wait(barrier, len(peers))
    tell(0)
    send(g_give, g_take, v_sems, 1, other_core)
    g_copy = sending(g_take, v_sems, 1)
    send(v_ref, v_other, v_sems, 0, other_core)
    v_copy = sending(v_other, v_sems, 0)
    inputs[1].wait()
    a_value = a_ref[...]
    gap = jnp.zeros((ROWS, NB - SHARD), F32)
    for s in range(8):
        first, second = s * 2 * SHARD, (s * 2 + 1) * SHARD
        pieces = [
            a_value[:, first : first + HALF],
            a_value[:, second : second + HALF],
            a_value[:, first + HALF : first + SHARD],
            gap,
            a_value[:, second + HALF : second + SHARD],
            gap,
        ]
        a_send[s] = jnp.concatenate(pieces, axis=1)
    a_recv[chip] = a_send[chip]
    for gy, gx, _ in group[1:-1:2]:
        where = (row, gy * 4 + gx * 2 + core)
        send(a_send.at[gy * 2 + gx], a_recv.at[chip], a_sems, 0, where)
    a_copies = sending(a_recv.at[pl.ds(0, 7)], a_sems, 0)

    def v_parts(b):
        return v_up[b].reshape(2 * NB, NB), v_low[b].reshape(2 * NB, NB)

    def start_first(half, part, into, sems):
        for d, place, peer in (y_peers, x_peers)[half]:
            src = part.at[0, :, place] if half == 0 else part.at[1, :, :, place]
            send(src, into.at[half, d - 1], sems, half, peer)
        return sending(into.at[half], sems, half)

    def finish_first(half, copies, part, into, mid):
        wait_bytes(*copies)
        own = part[0, :, y] if half == 0 else part[1, :, :, x]
        mid[half] = own + into[half, 0] + into[half, 1] + into[half, 2]

    def start_second(half, mid, into, sems):
        for d, place, peer in (x_peers, y_peers)[half]:
            send(mid.at[half, :, place], into.at[half, d - 1], sems, half, peer)
        return sending(into.at[half], sems, half)

    def finish_second(half, copies, mid, into, tiles):
        wait_bytes(*copies)
        value = mid[half, :, (x, y)[half]] + into[half, 0] + into[half, 1] + into[half, 2]
        count, lanes = value.shape[0], value.shape[2] // 128
        for t in range(count * 2 * lanes):
            j, g, h = t // (2 * lanes), t // lanes % 2, t % lanes
            piece = value[j, g * 8 : g * 8 + 8, h * 128 : h * 128 + 128]
            tiles[half * count * 2 * lanes + t] = piece

    def start_z(tiles, into, sems):
        for d, place, peer in z_peers:
            send(tiles.at[place], into.at[d - 1], sems, 0, peer)
        return sending(into, sems, 0)

    def finish_z(copies, tiles, into, own):
        wait_bytes(*copies)
        own[z] = tiles[z] + jnp.sum(into[...], axis=0)

    def start_z_back(own, sems):
        for _, _, peer in z_peers:
            send(own.at[z], own.at[z], sems, 0, peer)
        return sending(own.at[pl.ds(0, ZN - 1)], sems, 0)

    def finish_z_back(copies, own, count, lanes):
        wait_bytes(*copies)
        blocks = []
        for j in range(2 * count):
            base = j * 2 * lanes
            halves = [
                jnp.concatenate([own[base + g * lanes + h] for h in range(lanes)], axis=1)
                for g in range(2)
            ]
            blocks.append(jnp.concatenate(halves, axis=0))
        return blocks

    def start_back(half, whole, sems):
        mine = whole.at[half, :, y, x]
        for _, _, peer in (x_peers, y_peers)[half]:
            send(mine, mine, sems, half, peer)
        return sending(whole.at[half, :, 0, pl.ds(0, 3)], sems, half)

    def finish_back(half, whole, copies, sems):
        wait_bytes(*copies)
        mine = whole.at[0, :, y] if half == 0 else whole.at[1, :, :, x]
        for _, _, peer in (y_peers, x_peers)[half]:
            send(mine, mine, sems, half, peer)
        return sending(whole.at[half, :, pl.ds(0, 3)], sems, half)

    wait_bytes(*g_copy)
    for j in range(PAIRS):
        product = g_keep[j] + g_take[j]
        for half in range(2):
            lanes = product[:, half * 128 : half * 128 + 128]
            g_part[half, j] = lanes.reshape(YN, XN, 16, 128)
    g1 = [start_first(half, g_part, g_in1, g1_sems) for half in range(2)]
    hear(0)
    tell(1)
    wait_bytes(*v_copy)
    for b in range(BLOCKS):
        up, low = split_parts(padded(v_other[b]))
        v_up[b, :, 1 - core] = up
        v_low[b, :, 1 - core] = low
    hear(1)
    tell(2)

    g2 = []
    for half in range(2):
        finish_first(half, g1[half], g_part, g_in1, g_mid)
        g2.append(start_second(half, g_mid, g_in2, g2_sems))

    wait_bytes(*a_copies)
    a_parts = split_parts(a_recv[...].reshape(8 * ROWS, 2 * NB))
    p1 = []
    for half in range(2):
        for i in range(2):
            product = split_dot(a_parts, v_parts(3 - 2 * half - i), PLAIN)
            p_part[half, i] = product.reshape(YN, XN, 16, NB)
        p1.append(start_first(half, p_part, p_in1, p1_sems))

    for half in range(2):
        finish_second(half, g2[half], g_mid, g_in2, g_tiles)
    for t in range(12, ZN):
        g_tiles[t] = jnp.zeros((8, 128), F32)
    hear(2)
    g3 = start_z(g_tiles, g_in3, g3_sems)

    inputs[2].wait()
    for b in range(BLOCKS):
        up, low = split_parts(f_ref[b])
        f_up[b] = up
        f_low[b] = low
    inputs[3].wait()

    @pl.loop(0, 16 * ROWS, unroll=8)
    def _(k):
        source = order_ref[k]
        place_ref[k] = (source >> 5 & 1) * (8 * ROWS) + (source >> 6) * ROWS + (source & 31)

    p2 = []
    for half in range(2):
        finish_first(half, p1[half], p_part, p_in1, p_mid)
        p2.append(start_second(half, p_mid, p_in2, p2_sems))
    finish_z(g3, g_tiles, g_in3, g_own)
    g4 = start_z_back(g_own, g4_sems)
    for half in range(2):
        finish_second(half, p2[half], p_mid, p_in2, p_tiles)
    p3 = start_z(p_tiles, p_in3, p3_sems)

    g_mine = g_all.at[core]
    for j, block in enumerate(finish_z_back(g4, g_own, PAIRS, 1)):
        g_all[core, j // PAIRS, j % PAIRS, y, x] = block
    g5 = [start_back(half, g_mine, g5_sems) for half in range(2)]
    finish_z(p3, p_tiles, p_in3, p_own)
    p4 = start_z_back(p_own, p4_sems)
    g6 = [finish_back(half, g_mine, g5[half], g6_sems) for half in range(2)]

    for i, block in enumerate(finish_z_back(p4, p_own, 2, 2)):
        p_all[i // 2, i % 2, y, x] = block
    p5 = [start_back(half, p_all, p5_sems) for half in range(2)]
    g7 = []
    for half in range(2):
        wait_bytes(*g6[half])
        send(g_mine.at[half], g_mine.at[half], g7_sems, half, other_core)
        g7.append(sending(g_mine.at[half], g7_sems, half))
    p6 = [finish_back(half, p_all, p5[half], p6_sems) for half in range(2)]

    for part in range(2):
        o_part[part] = a_recv[:, :, part * NB : part * NB + NB].reshape(8 * ROWS, NB)

    def projected(i):
        return p_all[i // 2, i % 2].reshape(8 * ROWS, NB)

    def combine(value, i):
        return split_parts(split_dot(split_parts(value), (f_up[3 - i], f_low[3 - i]), RIGHT))

    def subtract(i, part):
        v_block = (v_up[3 - i, part].reshape(NB, NB), v_low[3 - i, part].reshape(NB, NB))
        return o_part[part] - split_dot(w_parts[i], v_block, RIGHT)

    wait_bytes(*p6[0])
    w_parts = [combine(projected(0), 0)]
    for part in range(2):
        o_part[part] = subtract(0, part)
    for copy in g7:
        wait_bytes(*copy)
    wait_bytes(*p6[1])

    def g_parts(c, j):
        block = jnp.concatenate(
            [g_all[c, half, j].reshape(NB, 128) for half in range(2)], axis=1
        )
        return split_parts(block)

    places = {(0, 1): (0, 0), (0, 2): (0, 1), (1, 2): (0, 2), (0, 3): (1, 0), (1, 3): (1, 1), (2, 3): (1, 2)}
    for i in range(1, BLOCKS):
        value = projected(i)
        for k in range(i):
            value = value - split_dot(w_parts[k], g_parts(*places[k, i]), PLAIN)
        w_parts.append(combine(value, i))
        if i < BLOCKS - 1:
            for part in range(2):
                o_part[part] = subtract(i, part)

    o_both = (o_both0, o_both1)
    oc = []
    for part in range(2):
        value = subtract(BLOCKS - 1, part)
        for side in range(2):
            o_sides[part, side] = value[:, side * HALF : side * HALF + HALF]
        into = o_both[part].at[pl.ds(core * 8 * ROWS, 8 * ROWS)]
        send(o_sides.at[part, 1 - core], into, oc_sems, part, other_core)
        oc.append(sending(o_sides.at[part, 1 - core], oc_sems, part))
        o_both[part][pl.ds(core * 8 * ROWS, 8 * ROWS)] = o_sides[part, core]
    o_copies = []
    for part in range(2):
        wait_bytes(*oc[part])
        for i, (ty, tx, tc) in enumerate(group):
            target = ty * 4 + tx * 2 + tc

            @pl.loop(0, ROWS, unroll=16)
            def _(k):
                place = place_ref[target * ROWS + k]
                o_send[part, target, pl.ds(k, 1), :] = o_both[part][pl.ds(place, 1), :]

            if i < 15:
                src, dst = o_send.at[part, target], o_recv.at[part, col]
                send(src, dst, o_sems, part, (row, target))
        o_copies.append(sending(o_recv.at[part, pl.ds(0, 15)], o_sems, part))
    for part in range(2):
        o_recv[part, col] = o_send[part, col]
    wait_sent()
    for copy in o_copies:
        wait_bytes(*copy)
    for c in range(16):
        out_ref[:, c * SHARD : c * SHARD + HALF] = o_recv[0, c]
        out_ref[:, c * SHARD + HALF : c * SHARD + SHARD] = o_recv[1, c][:, : SHARD - HALF]


def vmem(*shape):
    return pltpu.VMEM(shape, F32)


def half_vmem(*shape):
    return pltpu.VMEM(shape, BF16)


def sems(count):
    return pltpu.SemaphoreType.DMA((2, count))


def reduce_bufs(n, lanes):
    return [
        vmem(2, n, YN, XN, 16, lanes), vmem(2, 3, n, 4, 16, lanes), vmem(2, n, 4, 16, lanes),
        vmem(2, 3, n, 16, lanes), vmem(ZN, 8, 128), vmem(ZN - 1, 8, 128), vmem(ZN, 8, 128),
    ]


def per_device(merged_vectors, deflation, vectors, factors):
    rows = 8 * ROWS
    scratch = [
        pltpu.SMEM(deflation.shape, jnp.int32), pltpu.SMEM(deflation.shape, jnp.int32),
        vmem(*merged_vectors.shape),
        vmem(*vectors.shape), vmem(*factors.shape),
        vmem(BLOCKS, SHARD, NB),
        half_vmem(BLOCKS, 2, 2, HALF, NB), half_vmem(BLOCKS, 2, 2, HALF, NB),
        half_vmem(BLOCKS, NB, NB), half_vmem(BLOCKS, NB, NB),
        vmem(8, ROWS, 2 * NB), vmem(8, ROWS, 2 * NB),
        *reduce_bufs(2, NB),
        *reduce_bufs(PAIRS, 128),
        vmem(PAIRS, NB, NB), vmem(PAIRS, NB, NB), vmem(PAIRS, NB, NB),
        vmem(2, 2, PAIRS, YN, XN, 16, 128),
        vmem(2, 2, YN, XN, 16, NB),
        vmem(2, rows, NB), vmem(2, 2, rows, HALF), vmem(2 * rows, HALF), vmem(2 * rows, HALF),
        vmem(2, 16, ROWS, HALF), vmem(2, 16, ROWS, HALF),
        pltpu.SemaphoreType.DMA((4,)),
        sems(2), sems(1), sems(2), sems(2), sems(1), sems(1),
        sems(2), sems(2), sems(1), sems(1), sems(2), sems(2), sems(2),
        sems(2), sems(2), sems(2), sems(2), pltpu.SemaphoreType.REGULAR((3,)),
    ]
    in_place = pl.BlockSpec(memory_space=pltpu.HBM)
    return pl.pallas_call(
        kernel,
        out_shape=jax.ShapeDtypeStruct(merged_vectors.shape, F32),
        in_specs=[in_place] * 4,
        out_specs=pl.BlockSpec(memory_space=pltpu.VMEM),
        scratch_shapes=scratch,
        compiler_params=pltpu.CompilerParams(
            collective_id=0, has_side_effects=True, vmem_limit_bytes=427 * 128 * 1024
        ),
        name="back_transform",
    )(deflation, merged_vectors, vectors, factors)


def solution(mesh):
    in_specs = (P("col", "row"), P(), P(None, ("row", "col"), None), P())
    out_specs = P("col", "row")
    return jax.shard_map(
        per_device, mesh=mesh, in_specs=in_specs, out_specs=out_specs, check_vma=False
    )
```

```python
import jax
import jax.numpy as jnp
from jax import lax
from jax.experimental import pallas as pl
from jax.experimental.pallas import tpu as pltpu
from jax.sharding import PartitionSpec as P

MESH = pl.DeviceIdType.MESH
F32, BF16 = jnp.float32, jnp.bfloat16
YN, XN, ZN = 4, 4, 16
NB = 256
BLOCKS = 4
ROWS = 32
SHARD = 200
HALF = 128
PAIRS = 3
PLAIN = (((1,), (0,)), ((), ()))
RIGHT = (((1,), (1,)), ((), ()))
LEFT = (((0,), (0,)), ((), ()))


def split_parts(values):
    upper = values.astype(BF16)
    return upper, (values - upper.astype(F32)).astype(BF16)


def dot(a, b, numbers):
    return lax.dot_general(a, b, numbers, preferred_element_type=F32)


def split_dot(a, b, numbers):
    return dot(a[0], b[0], numbers) + dot(a[0], b[1], numbers) + dot(a[1], b[0], numbers)


def device(z, x, y, core):
    return (z * 2 + x // 2, y * 4 + (x % 2) * 2 + core)


def send(src, dst, sems, index, where):
    pltpu.make_async_remote_copy(
        src_ref=src,
        dst_ref=dst,
        send_sem=sems.at[0, index],
        recv_sem=sems.at[1, index],
        device_id=where,
        device_id_type=MESH,
    ).start()


def wait_bytes(like, sem):
    pltpu.make_async_copy(like, like, sem).wait()


def padded(values):
    rows = jnp.concatenate([values, jnp.zeros((NB - SHARD, values.shape[1]), F32)], axis=0)
    return rows.reshape(2, HALF, values.shape[1])


def kernel(
    order_hbm, a_hbm, v_hbm, f_hbm, out_ref,
    order_ref, place_ref, a_ref, v_ref, f_ref,
    v_other, v_up, v_low, f_up, f_low,
    a_send, a_recv,
    p_part, p_in1, p_mid, p_in2, p_tiles, p_in3, p_own,
    g_part, g_in1, g_mid, g_in2, g_tiles, g_in3, g_own,
    g_give, g_keep, g_take, g_all, p_all, o_part, o_sides, o_both0, o_both1, o_send, o_recv,
    in_sems, v_sems, a_sems, p1_sems, p2_sems, p3_sems, p4_sems,
    g1_sems, g2_sems, g3_sems, g4_sems, g5_sems, g6_sems, g7_sems,
    p5_sems, p6_sems, oc_sems, o_sems, known_sems,
):
    row = lax.axis_index("row")
    col = lax.axis_index("col")
    z, y, core = row // 2, col // 4, col % 2
    x_low = (col // 2) % 2
    x = (row % 2) * 2 + x_low
    chip = y * 2 + x_low
    sent = []

    def sending(like, sems, index):
        sent.append((like, sems.at[0, index]))
        return like, sems.at[1, index]

    def wait_sent():
        for like, sem in sent:
            wait_bytes(like, sem)
        sent.clear()

    y_peers = [(d, (y + d) % YN, device(z, x, (y + d) % YN, core)) for d in (2, 1, 3)]
    x_peers = [(d, (x + d) % XN, device(z, (x + d) % XN, y, core)) for d in (2, 1, 3)]
    far_first = sorted(range(1, ZN), key=lambda d: -min(d, ZN - d))
    z_peers = [(d, (z + d) % ZN, device((z + d) % ZN, x, y, core)) for d in far_first]
    group = []
    for dy in (2, 1, 3, 0):
        for dx in (1, 0):
            for dc in (1, 0):
                group.append(((y + dy) % YN, (x_low + dx) % 2, (core + dc) % 2))
    col_peers = [(row, gy * 4 + gx * 2 + gc) for gy, gx, gc in group[:-1]]
    far_x = [device(z, (x // 2 * 2 + 2) % XN + h, y, core) for h in range(2)]
    other_core = (row, y * 4 + x_low * 2 + 1 - core)

    barrier = pltpu.get_barrier_semaphore()
    near_z = [device((z + d) % ZN, x, y, core) for d in (1, ZN - 1)]
    peers = col_peers + far_x + near_z
    for peer in peers:
        pl.semaphore_signal(barrier, inc=1, device_id=peer, device_id_type=MESH)

    def tell(step):
        for d in (1 << step, ZN - (1 << step)):
            where = device((z + d) % ZN, x, y, core)
            pl.semaphore_signal(known_sems.at[step], inc=1, device_id=where, device_id_type=MESH)

    def hear(step):
        pl.semaphore_wait(known_sems.at[step], 2)

    inputs = [
        pltpu.make_async_copy(src, dst, in_sems.at[i])
        for i, (src, dst) in enumerate(
            ((v_hbm, v_ref), (a_hbm, a_ref), (f_hbm, f_ref), (order_hbm, order_ref))
        )
    ]
    for copy in inputs:
        copy.start()

    inputs[0].wait()
    for b in range(BLOCKS):
        up, low = split_parts(padded(v_ref[b]))
        v_up[b, :, core] = up
        v_low[b, :, core] = low

    def own_parts(b):
        return v_up[b, :, core].reshape(NB, NB), v_low[b, :, core].reshape(NB, NB)

    for to, into in ((1 - core, g_give), (core, g_keep)):
        lefts = (3, 3 - to, 2 - to)
        rights = (2 - 2 * to, 1 - to, 1 - to)
        for j in range(PAIRS):
            into[j] = split_dot(own_parts(lefts[j]), own_parts(rights[j]), LEFT)
    pl.semaphore_wait(barrier, len(peers))
    tell(0)
    send(g_give, g_take, v_sems, 1, other_core)
    g_copy = sending(g_take, v_sems, 1)
    inputs[1].wait()
    a_value = a_ref[...]
    gap = jnp.zeros((ROWS, NB - SHARD), F32)
    for s in range(8):
        first, second = s * 2 * SHARD, (s * 2 + 1) * SHARD
        pieces = [
            a_value[:, first : first + HALF],
            a_value[:, second : second + HALF],
            a_value[:, first + HALF : first + SHARD],
            gap,
            a_value[:, second + HALF : second + SHARD],
            gap,
        ]
        a_send[s] = jnp.concatenate(pieces, axis=1)
    a_recv[chip] = a_send[chip]
    for gy, gx, _ in group[1:-1:2]:
        where = (row, gy * 4 + gx * 2 + core)
        send(a_send.at[gy * 2 + gx], a_recv.at[chip], a_sems, 0, where)
    a_copies = sending(a_recv.at[pl.ds(0, 7)], a_sems, 0)

    def v_parts(b):
        return v_up[b].reshape(2 * NB, NB), v_low[b].reshape(2 * NB, NB)

    def start_first(half, part, into, sems):
        for d, place, peer in (y_peers, x_peers)[half]:
            src = part.at[0, :, place] if half == 0 else part.at[1, :, :, place]
            send(src, into.at[half, d - 1], sems, half, peer)
        return sending(into.at[half], sems, half)

    def finish_first(half, copies, part, into, mid):
        wait_bytes(*copies)
        own = part[0, :, y] if half == 0 else part[1, :, :, x]
        mid[half] = own + into[half, 0] + into[half, 1] + into[half, 2]

    def start_second(half, mid, into, sems):
        for d, place, peer in (x_peers, y_peers)[half]:
            send(mid.at[half, :, place], into.at[half, d - 1], sems, half, peer)
        return sending(into.at[half], sems, half)

    def finish_second(half, copies, mid, into, tiles):
        wait_bytes(*copies)
        value = mid[half, :, (x, y)[half]] + into[half, 0] + into[half, 1] + into[half, 2]
        count, lanes = value.shape[0], value.shape[2] // 128
        for t in range(count * 2 * lanes):
            j, g, h = t // (2 * lanes), t // lanes % 2, t % lanes
            piece = value[j, g * 8 : g * 8 + 8, h * 128 : h * 128 + 128]
            tiles[half * count * 2 * lanes + t] = piece

    def start_z(tiles, into, sems):
        for d, place, peer in z_peers:
            send(tiles.at[place], into.at[d - 1], sems, 0, peer)
        return sending(into, sems, 0)

    def finish_z(copies, tiles, into, own):
        wait_bytes(*copies)
        own[z] = tiles[z] + jnp.sum(into[...], axis=0)

    def start_z_back(own, sems):
        for _, _, peer in z_peers:
            send(own.at[z], own.at[z], sems, 0, peer)
        return sending(own.at[pl.ds(0, ZN - 1)], sems, 0)

    def finish_z_back(copies, own, count, lanes):
        wait_bytes(*copies)
        blocks = []
        for j in range(2 * count):
            base = j * 2 * lanes
            halves = [
                jnp.concatenate([own[base + g * lanes + h] for h in range(lanes)], axis=1)
                for g in range(2)
            ]
            blocks.append(jnp.concatenate(halves, axis=0))
        return blocks

    def start_back(half, whole, sems):
        mine = whole.at[half, :, y, x]
        for _, _, peer in (x_peers, y_peers)[half]:
            send(mine, mine, sems, half, peer)
        return sending(whole.at[half, :, 0, pl.ds(0, 3)], sems, half)

    def finish_back(half, whole, copies, sems):
        wait_bytes(*copies)
        mine = whole.at[0, :, y] if half == 0 else whole.at[1, :, :, x]
        for _, _, peer in (y_peers, x_peers)[half]:
            send(mine, mine, sems, half, peer)
        return sending(whole.at[half, :, pl.ds(0, 3)], sems, half)

    wait_bytes(*g_copy)
    send(v_ref, v_other, v_sems, 0, other_core)
    v_copy = sending(v_other, v_sems, 0)
    for j in range(PAIRS):
        product = g_keep[j] + g_take[j]
        for half in range(2):
            lanes = product[:, half * 128 : half * 128 + 128]
            g_part[half, j] = lanes.reshape(YN, XN, 16, 128)
    g1 = [start_first(half, g_part, g_in1, g1_sems) for half in range(2)]
    hear(0)
    tell(1)
    wait_bytes(*v_copy)
    for b in range(BLOCKS):
        up, low = split_parts(padded(v_other[b]))
        v_up[b, :, 1 - core] = up
        v_low[b, :, 1 - core] = low
    hear(1)
    tell(2)

    g2 = []
    for half in range(2):
        finish_first(half, g1[half], g_part, g_in1, g_mid)
        g2.append(start_second(half, g_mid, g_in2, g2_sems))

    wait_bytes(*a_copies)
    a_parts = split_parts(a_recv[...].reshape(8 * ROWS, 2 * NB))
    p1 = []
    for half in range(2):
        for i in range(2):
            product = split_dot(a_parts, v_parts(3 - 2 * half - i), PLAIN)
            p_part[half, i] = product.reshape(YN, XN, 16, NB)
        p1.append(start_first(half, p_part, p_in1, p1_sems))

    for half in range(2):
        finish_second(half, g2[half], g_mid, g_in2, g_tiles)
    for t in range(12, ZN):
        g_tiles[t] = jnp.zeros((8, 128), F32)
    hear(2)
    g3 = start_z(g_tiles, g_in3, g3_sems)

    inputs[2].wait()
    for b in range(BLOCKS):
        up, low = split_parts(f_ref[b])
        f_up[b] = up
        f_low[b] = low
    inputs[3].wait()

    @pl.loop(0, 16 * ROWS, unroll=8)
    def _(k):
        source = order_ref[k]
        place_ref[k] = (source >> 5 & 1) * (8 * ROWS) + (source >> 6) * ROWS + (source & 31)

    p2 = []
    for half in range(2):
        finish_first(half, p1[half], p_part, p_in1, p_mid)
        p2.append(start_second(half, p_mid, p_in2, p2_sems))
    finish_z(g3, g_tiles, g_in3, g_own)
    g4 = start_z_back(g_own, g4_sems)
    for half in range(2):
        finish_second(half, p2[half], p_mid, p_in2, p_tiles)
    p3 = start_z(p_tiles, p_in3, p3_sems)

    g_mine = g_all.at[core]
    for j, block in enumerate(finish_z_back(g4, g_own, PAIRS, 1)):
        g_all[core, j // PAIRS, j % PAIRS, y, x] = block
    g5 = [start_back(half, g_mine, g5_sems) for half in range(2)]
    finish_z(p3, p_tiles, p_in3, p_own)
    p4 = start_z_back(p_own, p4_sems)
    g6 = [finish_back(half, g_mine, g5[half], g6_sems) for half in range(2)]

    for i, block in enumerate(finish_z_back(p4, p_own, 2, 2)):
        p_all[i // 2, i % 2, y, x] = block
    p5 = [start_back(half, p_all, p5_sems) for half in range(2)]
    g7 = []
    for half in range(2):
        wait_bytes(*g6[half])
        send(g_mine.at[half], g_mine.at[half], g7_sems, half, other_core)
        g7.append(sending(g_mine.at[half], g7_sems, half))
    p6 = [finish_back(half, p_all, p5[half], p6_sems) for half in range(2)]

    for part in range(2):
        o_part[part] = a_recv[:, :, part * NB : part * NB + NB].reshape(8 * ROWS, NB)

    def projected(i):
        return p_all[i // 2, i % 2].reshape(8 * ROWS, NB)

    def combine(value, i):
        return split_parts(split_dot(split_parts(value), (f_up[3 - i], f_low[3 - i]), RIGHT))

    def subtract(i, part):
        v_block = (v_up[3 - i, part].reshape(NB, NB), v_low[3 - i, part].reshape(NB, NB))
        return o_part[part] - split_dot(w_parts[i], v_block, RIGHT)

    wait_bytes(*p6[0])
    w_parts = [combine(projected(0), 0)]
    for part in range(2):
        o_part[part] = subtract(0, part)
    for copy in g7:
        wait_bytes(*copy)
    wait_bytes(*p6[1])

    def g_parts(c, j):
        block = jnp.concatenate(
            [g_all[c, half, j].reshape(NB, 128) for half in range(2)], axis=1
        )
        return split_parts(block)

    places = {(0, 1): (0, 0), (0, 2): (0, 1), (1, 2): (0, 2), (0, 3): (1, 0), (1, 3): (1, 1), (2, 3): (1, 2)}
    for i in range(1, BLOCKS):
        value = projected(i)
        for k in range(i):
            value = value - split_dot(w_parts[k], g_parts(*places[k, i]), PLAIN)
        w_parts.append(combine(value, i))
        if i < BLOCKS - 1:
            for part in range(2):
                o_part[part] = subtract(i, part)

    o_both = (o_both0, o_both1)
    oc = []
    for part in range(2):
        value = subtract(BLOCKS - 1, part)
        for side in range(2):
            o_sides[part, side] = value[:, side * HALF : side * HALF + HALF]
        into = o_both[part].at[pl.ds(core * 8 * ROWS, 8 * ROWS)]
        send(o_sides.at[part, 1 - core], into, oc_sems, part, other_core)
        oc.append(sending(o_sides.at[part, 1 - core], oc_sems, part))
        o_both[part][pl.ds(core * 8 * ROWS, 8 * ROWS)] = o_sides[part, core]
    o_copies = []
    for part in range(2):
        wait_bytes(*oc[part])
        for i, (ty, tx, tc) in enumerate(group):
            target = ty * 4 + tx * 2 + tc

            @pl.loop(0, ROWS, unroll=16)
            def _(k):
                place = place_ref[target * ROWS + k]
                o_send[part, target, pl.ds(k, 1), :] = o_both[part][pl.ds(place, 1), :]

            if i < 15:
                src, dst = o_send.at[part, target], o_recv.at[part, col]
                send(src, dst, o_sems, part, (row, target))
        o_copies.append(sending(o_recv.at[part, pl.ds(0, 15)], o_sems, part))
    for part in range(2):
        o_recv[part, col] = o_send[part, col]
    wait_sent()
    for copy in o_copies:
        wait_bytes(*copy)
    for c in range(16):
        out_ref[:, c * SHARD : c * SHARD + HALF] = o_recv[0, c]
        out_ref[:, c * SHARD + HALF : c * SHARD + SHARD] = o_recv[1, c][:, : SHARD - HALF]


def vmem(*shape):
    return pltpu.VMEM(shape, F32)


def half_vmem(*shape):
    return pltpu.VMEM(shape, BF16)


def sems(count):
    return pltpu.SemaphoreType.DMA((2, count))


def reduce_bufs(n, lanes):
    return [
        vmem(2, n, YN, XN, 16, lanes), vmem(2, 3, n, 4, 16, lanes), vmem(2, n, 4, 16, lanes),
        vmem(2, 3, n, 16, lanes), vmem(ZN, 8, 128), vmem(ZN - 1, 8, 128), vmem(ZN, 8, 128),
    ]


def per_device(merged_vectors, deflation, vectors, factors):
    rows = 8 * ROWS
    scratch = [
        pltpu.SMEM(deflation.shape, jnp.int32), pltpu.SMEM(deflation.shape, jnp.int32),
        vmem(*merged_vectors.shape),
        vmem(*vectors.shape), vmem(*factors.shape),
        vmem(BLOCKS, SHARD, NB),
        half_vmem(BLOCKS, 2, 2, HALF, NB), half_vmem(BLOCKS, 2, 2, HALF, NB),
        half_vmem(BLOCKS, NB, NB), half_vmem(BLOCKS, NB, NB),
        vmem(8, ROWS, 2 * NB), vmem(8, ROWS, 2 * NB),
        *reduce_bufs(2, NB),
        *reduce_bufs(PAIRS, 128),
        vmem(PAIRS, NB, NB), vmem(PAIRS, NB, NB), vmem(PAIRS, NB, NB),
        vmem(2, 2, PAIRS, YN, XN, 16, 128),
        vmem(2, 2, YN, XN, 16, NB),
        vmem(2, rows, NB), vmem(2, 2, rows, HALF), vmem(2 * rows, HALF), vmem(2 * rows, HALF),
        vmem(2, 16, ROWS, HALF), vmem(2, 16, ROWS, HALF),
        pltpu.SemaphoreType.DMA((4,)),
        sems(2), sems(1), sems(2), sems(2), sems(1), sems(1),
        sems(2), sems(2), sems(1), sems(1), sems(2), sems(2), sems(2),
        sems(2), sems(2), sems(2), sems(2), pltpu.SemaphoreType.REGULAR((3,)),
    ]
    in_place = pl.BlockSpec(memory_space=pltpu.HBM)
    return pl.pallas_call(
        kernel,
        out_shape=jax.ShapeDtypeStruct(merged_vectors.shape, F32),
        in_specs=[in_place] * 4,
        out_specs=pl.BlockSpec(memory_space=pltpu.VMEM),
        scratch_shapes=scratch,
        compiler_params=pltpu.CompilerParams(
            collective_id=0, has_side_effects=True, vmem_limit_bytes=427 * 128 * 1024
        ),
        name="back_transform",
    )(deflation, merged_vectors, vectors, factors)


def solution(mesh):
    in_specs = (P("col", "row"), P(), P(None, ("row", "col"), None), P())
    out_specs = P("col", "row")
    return jax.shard_map(
        per_device, mesh=mesh, in_specs=in_specs, out_specs=out_specs, check_vma=False
    )
```
